512 devices in a mesh: src: 32 (over y, x, core), tm: 16 (over z).
Axes of the slice: x: 4, y: 4, z: 16, core: 2. Of those that a mesh axis runs over, the one named last changes fastest.
Arguments:
- observed: float32 [16, 131072], P(None, ('src', 'tm')), may hold values from -8 to 8
- weight_obs: float32 [16, 131072], P(None, ('src', 'tm')), may hold values from 0.25 to 4
- present: int32 [16, 131072], P(None, ('src', 'tm')), may hold values 0 or 1
- source_partials: float32 [5, 16, 131072], P(None, None, ('src', 'tm')), may hold values from -6 to 6
- attitude_partials: float32 [4, 16, 131072], P(None, None, ('src', 'tm')), may hold values from -6 to 6
- phase: float32 [16, 131072], P(None, ('src', 'tm')), may hold values from 0 to 1
- knot_base: int32 [16, 131072], P(None, ('src', 'tm')), may hold values from 0 to 28
- source_id: int32 [16, 131072], P(None, ('src', 'tm')), may hold values from 0 to 127, as said below
- cal_id: int32 [16, 131072], P(None, ('src', 'tm')), may hold values from 0 to 32767
- attitude: float32 [2048], P('tm'), may hold values from -4 to 4
- calibration: float32 [32768], replicated, may hold values from -4 to 4
Outputs:
- source_params: float32 [5, 65536], P(None, ('src', 'tm'))
- attitude_out: float32 [2048], P('tm')
- calibration_out: float32 [32768], replicated
- residual: float32 [16, 131072], P(None, ('src', 'tm'))
The draws below stay inside these ranges and needn't reach their ends.
Inputs may be any that keep to these rules, and one draw needn't show every extreme that they name: `source_id`: within each device's block of 256 columns the ids name that device's 128 sources, each of them at least once.
All inputs are finite; a program needn't handle non-finite values. No bound on the sum of `present` on one device may be relied on, other than what follows from the above.
Results may differ from the reference program's by a relative error of at most 0.0003.
Values sent between devices are 32-bit elements; how exact they have to be, the bound alone decides.
A program may use at most 64 MiB of HBM per device.

```python
import math
import jax
import jax.numpy as jnp
from jax import lax

KNOTS_DEV = 32
SRC_DEV = 128
SLOT = 256
CAL = 32768
ITERS = 2
SOURCES = 65536
OBS_COLS = 131072
ATT = 2048
N_TM = 16


def draw_source_id(key, part):
    key = jax.random.fold_in(key, 11)
    holders = SOURCES // SRC_DEV
    per_holder = N_TM * SLOT
    perm_keys = jax.random.split(jax.random.fold_in(key, 1), holders)
    orders = jax.vmap(lambda single: jax.random.permutation(single, SRC_DEV))(perm_keys)
    rest = jax.random.randint(jax.random.fold_in(key, 2), (holders, per_holder - SRC_DEV), 0, SRC_DEV)
    joined = jnp.concatenate([orders.astype(jnp.int32), rest.astype(jnp.int32)], axis=1)
    shuffle_keys = jax.random.split(jax.random.fold_in(key, 3), holders)
    mixed = jax.vmap(lambda single, values: jax.random.permutation(single, values))(shuffle_keys, joined)
    mixed = mixed.reshape(holders, N_TM, SLOT)
    return jnp.transpose(mixed, (1, 0, 2)).reshape(N_TM, holders * SLOT).astype(jnp.int32)


def touch_ends(values, own_key, smallest, top_value):
    place = [jax.random.randint(jax.random.fold_in(own_key, axis), (), 0, length) for axis, length in enumerate(values.shape)]
    longest = values.shape.index(max(values.shape))
    neighbour = place[:longest] + [(place[longest] + 1) % values.shape[longest]] + place[longest + 1:]
    return values.at[tuple(place)].set(smallest).at[tuple(neighbour)].set(top_value)


def with_spikes(values, key, source, target, blocks, factor):
    owner, partner = [(jnp.arange(values.shape[axis_at]) // (values.shape[axis_at] // blocks)).reshape([-1 if axis == axis_at else 1 for axis in range(values.ndim)]) for axis_at in (source, target)]
    chosen = jax.random.permutation(key, blocks)[partner]
    strong = (owner == chosen) | (owner == (partner + blocks // 2) % blocks)
    return jnp.where(strong, factor * values, values)


def steps_of(stream_key, shape, shards, smallest, largest):
    level, own = 1.0, jax.random.fold_in(stream_key, 6)
    for dim, parts in shards:
        heights = jnp.exp(jax.random.uniform(jax.random.fold_in(own, dim), (parts,), jnp.float32, smallest / len(shards), largest / len(shards)))
        level = level * jnp.repeat(heights, shape[dim] // parts).reshape([-1 if axis == dim else 1 for axis in range(len(shape))])
    return level


def bell_draw(rng, dims, spread, limit, pieces=(), kind=jnp.bfloat16):
    drawn = jax.random.normal(rng, dims, jnp.float32) * spread
    if len(pieces) > 0:
        drawn = steps_of(rng, dims, pieces, -0.22, 0.18) * drawn
    return jnp.clip(drawn, min=-limit, max=limit).astype(kind)


def noise_with(key, dims, deviation, bound, shards, heavy, kind=jnp.bfloat16):
    values = deviation * jax.random.normal(key, dims, jnp.float32)
    if shards:
        values = values * steps_of(key, dims, shards, -0.22, 0.18)
    return jnp.clip(with_spikes(values, jax.random.fold_in(key, 3), *heavy), -bound, bound).astype(kind)


def setup_inputs(seed: int = 0) -> dict:
    arg_keys = jax.random.split(jax.random.key(seed), 12)
    return {
        "observed": noise_with(arg_keys[0], (N_TM, OBS_COLS), 1.0, 8.0, ((1, 512),), (1, 0, 16, 2.0), jnp.float32),
        "weight_obs": jnp.clip(jnp.exp(math.log(4.0) - 2.7725887 * jax.random.uniform(arg_keys[1], (N_TM, OBS_COLS), jnp.float32) ** steps_of(arg_keys[1], (N_TM, OBS_COLS), ((1, 512),), -0.2, 0.2)), 0.25, 4.0),
        "present": touch_ends((jax.random.randint(arg_keys[2], (N_TM, OBS_COLS), 0, 4) < 3).astype(jnp.int32), jax.random.fold_in(arg_keys[2], 1), 0, 1),
        "source_partials": bell_draw(arg_keys[3], (5, N_TM, OBS_COLS), 1.0, 6.0, ((2, 512),), jnp.float32),
        "attitude_partials": bell_draw(arg_keys[4], (4, N_TM, OBS_COLS), 1.0, 6.0, ((2, 512),), jnp.float32),
        "phase": jnp.clip(1.0 * jax.random.uniform(arg_keys[5], (N_TM, OBS_COLS), jnp.float32) ** steps_of(arg_keys[5], (N_TM, OBS_COLS), ((1, 512),), -0.2, 0.2), 0.0, 1.0),
        "knot_base": touch_ends(jax.random.randint(arg_keys[6], (N_TM, OBS_COLS), 0, KNOTS_DEV - 3), jax.random.fold_in(arg_keys[6], 1), 0, (KNOTS_DEV - 3) - 1).astype(jnp.int32),
        "source_id": draw_source_id(jax.random.fold_in(arg_keys[11], 71), 0),
        "cal_id": touch_ends(jax.random.randint(arg_keys[8], (N_TM, OBS_COLS), 0, CAL), jax.random.fold_in(arg_keys[8], 1), 0, CAL - 1).astype(jnp.int32),
        "attitude": bell_draw(arg_keys[9], (ATT,), 0.5, 4.0, ((0, 16),), jnp.float32),
        "calibration": bell_draw(arg_keys[10], (CAL,), 0.5, 4.0, (), jnp.float32),
    }


PAIRS = [(row_id, col_id) for row_id in range(5) for col_id in range(row_id + 1)]

def spline_terms(phase, attitude_partials):
    other = 1.0 - phase
    square = phase * phase
    cube = square * phase
    basis = [other * other * other / 6.0, (3.0 * cube - 6.0 * square + 4.0) / 6.0, (-3.0 * cube + 3.0 * square + 3.0 * phase + 1.0) / 6.0, cube / 6.0]
    return jnp.stack([basis[knot_step] * attitude_partials[channel] for knot_step in range(4) for channel in range(4)])

def attitude_model(coefficients, terms, knot_base):
    table = coefficients.reshape(knot_base.shape[0], -1, 4)
    running = jnp.zeros(knot_base.shape, jnp.float32)
    for knot_step in range(4):
        for channel in range(4):
            picked = jnp.take_along_axis(table[:, :, channel], knot_base + knot_step, axis=1)
            running = running + terms[4 * knot_step + channel] * picked
    return running

def small_solve(matrix, right_side):
    extent = len(right_side)
    factor = {}
    for member in range(extent):
        for column in range(member + 1):
            running = matrix[member][column]
            for offset in range(column):
                running = running - factor[member, offset] * factor[column, offset]
            if member == column:
                factor[member, member] = jnp.sqrt(running)
            else:
                factor[member, column] = running / factor[column, column]
    forward = []
    for member in range(extent):
        running = right_side[member]
        for offset in range(member):
            running = running - factor[member, offset] * forward[offset]
        forward.append(running / factor[member, member])
    result = [None] * extent
    for member in reversed(range(extent)):
        running = forward[member]
        for offset in range(member + 1, extent):
            running = running - factor[offset, member] * result[offset]
        result[member] = running / factor[member, member]
    return jnp.stack(result)

def source_solve(ids, count, weighted, source_partials, target):
    products = [weighted * source_partials[row_id] * source_partials[col_id] for row_id, col_id in PAIRS]
    products = products + [weighted * source_partials[row_id] * target for row_id in range(5)]
    stacked = jnp.stack(products).reshape(len(products), -1).T
    sums = jax.ops.segment_sum(stacked, ids.reshape(-1), num_segments=count).T
    entries = {}
    for position, pair in enumerate(PAIRS):
        entry_value = sums[position] + (1.0 if pair[0] == pair[1] else 0.0)
        entries[pair[0], pair[1]] = entry_value
        entries[pair[1], pair[0]] = entry_value
    matrix = [[entries[row_id, col_id] for col_id in range(5)] for row_id in range(5)]
    return small_solve(matrix, [sums[15 + row_id] for row_id in range(5)])

def spd_solve(matrix, right_side):
    eye = jnp.eye(matrix.shape[-1], dtype=jnp.float32)
    lower = jnp.linalg.cholesky(matrix + eye)
    middle = lax.linalg.triangular_solve(lower, right_side[..., None], left_side=True, lower=True)
    result = lax.linalg.triangular_solve(lower, middle, left_side=True, lower=True, transpose_a=True)
    return result[..., 0]

def band_normals(terms, knot_base, weighted, resid):
    windows = KNOTS_DEV - 3
    width = 4 * KNOTS_DEV

    def single(item):
        part, base, weights, values = item
        outer = (part[:, None, :] * (weights[None, None, :] * part[None, :, :])).reshape(256, -1).T
        band = jax.ops.segment_sum(outer, base, num_segments=windows).reshape(windows, 16, 16)
        side = jax.ops.segment_sum((part * (weights * values)[None, :]).T, base, num_segments=windows)
        normal = jnp.zeros((width, width), jnp.float32)
        right = jnp.zeros((width,), jnp.float32)
        for start in range(windows):
            normal = normal.at[4 * start:4 * start + 16, 4 * start:4 * start + 16].add(band[start])
            right = right.at[4 * start:4 * start + 16].add(side[start])
        return (normal, right)
    return lax.map(single, (jnp.moveaxis(terms, 1, 0), knot_base, weighted, resid))

def reference(observed, weight_obs, present, source_partials, attitude_partials, phase, knot_base, source_id, cal_id, attitude, calibration):
    weighted = present.astype(jnp.float32) * weight_obs
    terms = spline_terms(phase, attitude_partials)
    holders = lax.broadcasted_iota(jnp.int32, source_id.shape, 1) // SLOT
    global_ids = (source_id + holders * SRC_DEV).astype(jnp.int32)
    current = attitude
    cal_now = calibration
    flat_cal = cal_id.reshape(-1)
    params = jnp.zeros((5, SOURCES), jnp.float32)
    for sweep in range(ITERS):
        target = observed - attitude_model(current, terms, knot_base) - cal_now[cal_id]
        params = source_solve(global_ids, SOURCES, weighted, source_partials, target)
        resid = target - lax.optimization_barrier(jnp.sum(source_partials * params[:, global_ids], axis=0))
        normals, rights = band_normals(terms, knot_base, weighted, resid)
        current = current + spd_solve(normals, rights).reshape(-1)
        numer = jax.ops.segment_sum((weighted * resid).reshape(-1), flat_cal, num_segments=CAL)
        denom = jax.ops.segment_sum(weighted.reshape(-1), flat_cal, num_segments=CAL)
        cal_now = cal_now + numer / (denom + 1.0)
    final = observed - attitude_model(current, terms, knot_base) - cal_now[cal_id]
    final = final - lax.optimization_barrier(jnp.sum(source_partials * params[:, global_ids], axis=0))
    return (params, current, cal_now, final)
```

```python
import functools

import jax
import jax.numpy as jnp
from jax import lax
from jax.experimental import pallas as pl
from jax.experimental.pallas import tpu as pltpu
from jax.sharding import PartitionSpec as P

MESH = pl.DeviceIdType.MESH
F32, BF16 = jnp.float32, jnp.bfloat16
ROWS, SLOT, SRC, KNOTS, LANES = 16, 256, 128, 32, 128
OBS = ROWS * SLOT
SHARD = 8
PAIRS = [(i, j) for i in range(5) for j in range(i + 1)]
TILES = [(i, h) for i in range(2) for h in range(2)]
NT = (((1,), (1,)), ((), ()))


def iota(shape, axis):
    return lax.broadcasted_iota(jnp.int32, shape, axis)


def loop(count, step, unroll=1):
    def body(at, carry):
        step(at)
        return carry

    lax.fori_loop(0, count, body, 0, unroll=unroll)


def split(value):
    head = value.astype(BF16).astype(F32)
    return head, value - head


def nt_dot(left, right):
    return lax.dot_general(left, right, NT, preferred_element_type=F32)


def whole(tiles):
    return jnp.concatenate(
        [jnp.concatenate([tiles[i, 0], tiles[i, 1]], axis=1) for i in range(2)], axis=0
    )


def tile(ref, i, h):
    return ref[8 * i : 8 * i + 8, 128 * h : 128 * h + 128]


def along(table, places):
    return jnp.take_along_axis(table, places, axis=1)


def wide(row, rows=8):
    return jnp.broadcast_to(row, (rows, row.shape[-1]))


def choose(rows, order):
    place = iota((8, rows[0].shape[-1]), 0)
    out = wide(rows[order[0]])
    for r in range(1, 8):
        if order[r] != order[r - 1]:
            out = jnp.where(place >= r, wide(rows[order[r]]), out)
    return out


def factor_of(entries):
    low, inv = {}, {}
    for i in range(5):
        for j in range(i + 1):
            rest = entries[i, j]
            for o in range(j):
                rest = rest - low[i, o] * low[j, o]
            if i == j:
                inv[i] = 1.0 / jnp.sqrt(rest)
            else:
                low[i, j] = rest * inv[j]
    return low, inv


def solve_with(low, inv, right):
    forward = []
    for i in range(5):
        rest = right[i]
        for o in range(i):
            rest = rest - low[i, o] * forward[o]
        forward.append(rest * inv[i])
    out = [None] * 5
    for i in reversed(range(5)):
        rest = forward[i]
        for o in range(i + 1, 5):
            rest = rest - low[o, i] * out[o]
        out[i] = rest * inv[i]
    return out


def band_place(shape):
    lane = iota(shape, 1)
    return iota(shape, 0) + 32 * (lane // 32) + lane % 4


def kernel(
    ns,
    nt,
    obs,
    wobs,
    pres,
    sp,
    ap,
    ph,
    kb,
    sid,
    cid,
    att,
    cal,
    params_o,
    att_o,
    cal_o,
    res_o,
    rows_s,
    dd,
    hot_hi,
    hot_src,
    units,
    lhs,
    matrix,
    fac,
    inv_den,
    qbuf,
    qsend,
    a1s,
    a1r,
    b1s,
    b1r,
    pair_r,
    a2s,
    a2r,
    b2s,
    b2r,
    c2s,
    c2r,
    a3s,
    a3r,
    b3s,
    b3r,
    c3s,
    c3r,
    send,
    recv,
):
    me_s, me_t = lax.axis_index("src"), lax.axis_index("tm")

    def to_src(stage, source, target, other, sender):
        return pltpu.make_async_remote_copy(
            src_ref=source,
            dst_ref=target,
            send_sem=send.at[stage, other],
            recv_sem=recv.at[stage, sender],
            device_id=(other, me_t),
            device_id_type=MESH,
        )

    def to_tm(stage, source, target, other, sender):
        return pltpu.make_async_remote_copy(
            src_ref=source,
            dst_ref=target,
            send_sem=send.at[stage, other],
            recv_sem=recv.at[stage, sender],
            device_id=(me_s, other),
            device_id_type=MESH,
        )

    def others(count, me, step):
        def body(d, carry):
            step(lax.rem(me + d, count))
            return carry

        lax.fori_loop(1, count, body, 0)

    def scatter_start(stage, source, target):
        others(
            ns, me_s, lambda o: to_src(stage, source.at[o], target.at[me_s], o, me_s).start()
        )
        target[me_s] = source[me_s]

    def scatter_wait(stage, source, target):
        def step(o):
            copy = to_src(stage, source.at[o], target.at[o], o, o)
            copy.wait_recv()

        others(ns, me_s, step)

    def scatter_sent(stage, source, target):
        others(
            ns,
            me_s,
            lambda o: to_src(stage, source.at[o], target.at[me_s], o, me_s).wait_send(),
        )

    def gather_start(stage, source, target, axis):
        count, me, to = (ns, me_s, to_src) if axis == "src" else (nt, me_t, to_tm)
        others(count, me, lambda o: to(stage, source, target.at[me], o, me).start())
        target[me] = source[...]

    def gather_wait(stage, source, target, axis):
        count, me, to = (ns, me_s, to_src) if axis == "src" else (nt, me_t, to_tm)
        others(count, me, lambda o: to(stage, source, target.at[o], o, o).wait_recv())

    def gather_sent(stage, source, target, axis):
        count, me, to = (ns, me_s, to_src) if axis == "src" else (nt, me_t, to_tm)
        others(count, me, lambda o: to(stage, source, target.at[me], o, me).wait_send())

    barrier = pltpu.get_barrier_semaphore()

    def greet_src(o):
        pl.semaphore_signal(barrier, inc=1, device_id=(o, me_t), device_id_type=MESH)

    def greet_tm(o):
        pl.semaphore_signal(barrier, inc=1, device_id=(me_s, o), device_id_type=MESH)

    others(ns, me_s, greet_src)
    others(nt, me_t, greet_tm)

    weight = pres[...].astype(F32) * wobs[...]
    root = jnp.sqrt(weight)
    u = ph[...]
    square = u * u
    cube = square * u
    other = 1.0 - u
    basis = [
        other * other * other / 6.0,
        (3.0 * cube - 6.0 * square + 4.0) / 6.0,
        (-3.0 * cube + 3.0 * square + 3.0 * u + 1.0) / 6.0,
        cube / 6.0,
    ]
    for j in range(4):
        rows_s[j] = basis[j] * root
        rows_s[4 + j] = basis[j]
    rows_s[8] = weight
    rows_s[9] = root
    w_hi, w_lo = split(weight)
    rows_s[10] = w_hi
    rows_s[11] = w_lo

    def row(at, k):
        return rows_s[at, pl.ds(k, 1), :]

    def lanes(k):
        return pl.ds(pl.multiple_of(k * SLOT, SLOT), SLOT)

    spread = band_place((ROWS, LANES))
    group = (iota((ROWS, LANES), 1) % 32) // 4

    def design_row(k):
        knot = iota((KNOTS, SLOT), 0) - wide(kb[pl.ds(k, 1), :], KNOTS)
        share = jnp.zeros((KNOTS, SLOT), F32)
        for j in range(4):
            share = jnp.where(knot == j, wide(row(j, k), KNOTS), share)
        for c in range(4):
            value = share * wide(ap[c, pl.ds(k, 1), :], KNOTS)
            head, tail = split(value)
            dd[k, 32 * c : 32 * c + 32, :] = head.astype(BF16)
            dd[k, 128 + 32 * c : 160 + 32 * c, :] = tail.astype(BF16)
        both = dd[k]
        full = nt_dot(both, both)
        normal = full[:128, :128] + full[:128, 128:] + full[128:, :128] + full[128:, 128:]
        packed = jnp.zeros((ROWS, LANES), F32)
        for g in range(8):
            part = along(normal[16 * g : 16 * g + 16], (spread + 16 * g) & 127)
            packed = jnp.where(group == g, part, packed)
        a1s[2 * k, 8:16, :] = packed[:8]
        a1s[2 * k + 1, 8:16, :] = packed[8:]

    loop(ROWS, design_row)

    def hot_row(k):
        ids = cid[pl.ds(k, 1), :]
        hit = iota((256, SLOT), 0) == wide(lax.shift_right_logical(ids, 7), 256)
        hot_hi[:, lanes(k)] = jnp.where(hit, 1.0, 0.0).astype(BF16)
        hit = iota((SRC, SLOT), 0) == wide(sid[pl.ds(k, 1), :], SRC)
        hot_src[:, lanes(k)] = jnp.where(hit, 1.0, 0.0).astype(BF16)

    loop(ROWS, hot_row)

    def unit_sums():
        def unit_row(k):
            low = cid[pl.ds(k, 1), :] & 127
            hit = iota((LANES, SLOT), 0) == wide(low, LANES)
            units[:128, lanes(k)] = jnp.where(hit, wide(row(10, k), LANES), 0.0).astype(BF16)
            units[128:, lanes(k)] = jnp.where(hit, wide(row(11, k), LANES), 0.0).astype(BF16)

        loop(ROWS, unit_row)
        both = nt_dot(hot_hi[...], units[...])
        return both[:, :128] + both[:, 128:]

    sums = unit_sums()
    for s in range(ns):
        a1s[s, 0:8, :] = sums[8 * s : 8 * s + 8]

    to_channel = iota((8, LANES), 1)
    to_channel = 4 * (to_channel % 32) + to_channel // 32
    qsend[...] = along(wide(att[...]), to_channel)[0:1]

    pl.semaphore_wait(barrier, ns + nt - 2)
    gather_start(0, qsend, qbuf, "tm")
    scatter_start(1, a1s, a1r)

    def source_row(k):
        a = [sp[i, pl.ds(k, 1), :] for i in range(5)]
        w = row(8, k)
        parts = []
        for first in (0, 8):
            chosen = (PAIRS + [(4, 4)])[first : first + 8]
            left = choose(a, [p[0] for p in chosen])
            parts.append(left * choose(a, [p[1] for p in chosen]) * wide(w))
        value = jnp.concatenate(parts, axis=0)
        head, tail = split(value)
        lhs[:16, lanes(k)] = head.astype(BF16)
        lhs[16:, lanes(k)] = tail.astype(BF16)

    loop(ROWS, source_row)
    sums = nt_dot(lhs[...], hot_src[...])
    sums = sums[:16] + sums[16:]
    entries = {}
    for at, (i, j) in enumerate(PAIRS):
        entries[i, j] = sums[at : at + 1] + (1.0 if i == j else 0.0)
    low, inv = factor_of(entries)
    keep = [low[i, j] for i, j in PAIRS if i != j] + [inv[i] for i in range(5)]
    for at, value in enumerate(keep):
        fac[at : at + 1] = value

    scatter_wait(1, a1s, a1r)
    b1s[...] = jnp.sum(a1r[...], axis=0)
    gather_start(2, b1s, b1r, "tm")

    def remaining(table, cal_tile):
        first = {t: jnp.zeros((8, LANES), F32) for t in TILES}
        low_id = {t: tile(cid, *t) & 127 for t in TILES}
        high_id = {t: lax.shift_right_logical(tile(cid, *t), 7) for t in TILES}

        def step(at, carry):
            carry = dict(zip(TILES, carry))
            block = cal_tile(at)
            for r in range(8):
                line = wide(block[r : r + 1])
                for t in TILES:
                    carry[t] = jnp.where(
                        high_id[t] == 8 * at + r, along(line, low_id[t]), carry[t]
                    )
            return tuple(carry[t] for t in TILES)

        got = lax.fori_loop(0, 32, step, tuple(first[t] for t in TILES))
        out = {}
        for t, offset in zip(TILES, got):
            i, h = t
            base = tile(kb, i, h)
            model = jnp.zeros((8, LANES), F32)
            for j in range(4):
                sum_c = jnp.zeros((8, LANES), F32)
                for c in range(4):
                    part = along(table[8 * i : 8 * i + 8], base + (32 * c + j))
                    sum_c = sum_c + tile(ap.at[c], i, h) * part
                model = model + tile(rows_s.at[4 + j], i, h) * sum_c
            out[t] = tile(obs, i, h) - model - offset
        return out

    def less_sources(target, params):
        out = {}
        for t in TILES:
            ids = tile(sid, *t)
            total = jnp.zeros((8, LANES), F32)
            for i in range(5):
                total = total + tile(sp.at[i], *t) * along(wide(params[i]), ids)
            out[t] = target[t] - total
        return out

    def solve_sources(target):
        rows_s[12] = rows_s[8] * whole(target)

        def side_row(k):
            a = [sp[i, pl.ds(k, 1), :] for i in range(5)]
            value = choose(a, [0, 1, 2, 3, 4, 4, 4, 4]) * wide(row(12, k))
            head, tail = split(value)
            lhs[:16, lanes(k)] = jnp.concatenate([head, tail], axis=0).astype(BF16)

        loop(ROWS, side_row)
        sums = nt_dot(lhs[:16, :], hot_src[...])
        sums = sums[:8] + sums[8:]
        kept = [fac[at : at + 1] for at in range(15)]
        low = dict(zip([p for p in PAIRS if p[0] != p[1]], kept[:10]))
        return solve_with(low, kept[10:], [sums[i : i + 1] for i in range(5)])

    def right_sides(resid, out):
        resid = whole(resid)
        value = rows_s[8] * resid
        head, tail = split(value)
        rows_s[10] = head
        rows_s[11] = tail
        sums = unit_sums()
        for s in range(ns):
            out[s, 0:8, :] = sums[8 * s : 8 * s + 8]
        head, tail = split(rows_s[9] * resid)
        left = jnp.concatenate([head, tail], axis=0).astype(BF16)
        for k in range(ROWS):
            got = nt_dot(left, dd[k])
            got = got[:, :128] + got[:, 128:]
            got = got[k : k + 1] + got[16 + k : 17 + k]
            out[2 * k, 8:9, :] = got
            out[2 * k + 1, 8:9, :] = got

    gather_wait(0, qsend, qbuf, "tm")
    table = jnp.concatenate([qbuf[k] for k in range(nt)], axis=0)
    target = remaining(table, lambda at: cal[pl.ds(pl.multiple_of(8 * at, 8), 8), :])
    params = solve_sources(target)
    right_sides(less_sources(target, params), a2s)
    scatter_start(3, a2s, a2r)

    gather_wait(2, b1s, b1r, "tm")
    summed = jnp.sum(b1r[...], axis=0)
    inv_den[...] = 1.0 / (1.0 + summed[0:8])
    half = lax.rem(me_s, 2)
    owned = me_s // 2
    b1s_sent = lambda: gather_sent(2, b1s, b1r, "tm")
    pair_r[half] = summed[8:16]
    partner = me_s + 1 - 2 * half
    swap = pltpu.make_async_remote_copy(
        src_ref=pair_r.at[half],
        dst_ref=pair_r.at[half],
        send_sem=send.at[9, 0],
        recv_sem=recv.at[9, 0],
        device_id=(partner, me_t),
        device_id_type=MESH,
    )
    swap.start()

    scatter_wait(3, a2s, a2r)
    b2s[...] = jnp.sum(a2r[...], axis=0)
    gather_start(4, b2s, b2r, "tm")

    swap.wait()
    packed = jnp.concatenate([pair_r[0], pair_r[1]], axis=0)
    lane = iota((ROWS, LANES), 1)
    for g in range(8):
        index = iota((ROWS, LANES), 0) + 16 * g
        ahead = (lane - index) & 127
        place = 32 * (ahead // 32) + 4 * g + ahead % 4
        matrix[16 * g : 16 * g + 16, :] = jnp.where(ahead % 32 < 4, along(packed, place), 0.0)
    upper = matrix[...]
    r_id, c_id = iota((128, 128), 0), iota((128, 128), 1)
    strict = jnp.where(r_id % 32 == c_id % 32, 0.0, upper)
    matrix[...] = upper + strict.T + jnp.where(r_id == c_id, 1.0, 0.0)

    def eliminate(i, carry):
        line = matrix[pl.ds(i, 1), :]
        here = iota((8, LANES), 1) == i
        at = jnp.zeros((8, LANES), jnp.int32) + i
        line = wide(line)
        pivot = 1.0 / along(line, at)
        scaled = jnp.where(here, pivot, line * pivot)
        for g in range(16):
            block = matrix[8 * g : 8 * g + 8, :]
            matrix[8 * g : 8 * g + 8, :] = jnp.where(here, 0.0, block) - along(block, at) * scaled
        matrix[pl.ds(i, 1), :] = scaled[0:1]
        return carry

    lax.fori_loop(0, 128, eliminate, 0)

    own_cal = pl.ds(pl.multiple_of(8 * me_s, 8), 8)

    def advance(now, later, offsets, q):
        got = jnp.sum(now[...], axis=0)
        later[0:8, :] = offsets + got[0:8] * inv_den[...]
        step = jnp.dot(
            wide(got[8:9]), matrix[...], precision=lax.Precision.HIGHEST, preferred_element_type=F32
        )
        later[8:9, :] = q + step[0:1]

    gather_wait(4, b2s, b2r, "tm")
    advance(b2r, c2s, cal[own_cal, :], qbuf[owned])
    gather_start(5, c2s, c2r, "src")
    gather_wait(5, c2s, c2r, "src")

    def table_of(got):
        return jnp.concatenate([got[2 * k, 8:9, :] for k in range(nt)], axis=0)

    target = remaining(table_of(c2r), lambda at: c2r[at, 0:8, :])
    params = solve_sources(target)
    for i in range(5):
        params_o[i : i + 1, :] = params[i]
    right_sides(less_sources(target, params), a3s)
    scatter_start(6, a3s, a3r)
    scatter_wait(6, a3s, a3r)
    b3s[...] = jnp.sum(a3r[...], axis=0)
    gather_start(7, b3s, b3r, "tm")
    gather_wait(7, b3s, b3r, "tm")
    advance(b3r, c3s, c2s[0:8, :], c2s[8:9, :])
    gather_start(8, c3s, c3r, "src")
    gather_wait(8, c3s, c3r, "src")

    table = table_of(c3r)
    target = remaining(table, lambda at: c3r[at, 0:8, :])
    res_o[...] = whole(less_sources(target, params))
    for s in range(ns):
        cal_o[8 * s : 8 * s + 8, :] = c3r[s, 0:8, :]
    to_knot = iota((8, LANES), 1)
    to_knot = 32 * (to_knot % 4) + to_knot // 4
    att_o[...] = along(wide(c3r[2 * me_t, 8:9, :]), to_knot)[0:1]

    gather_sent(0, qsend, qbuf, "tm")
    scatter_sent(1, a1s, a1r)
    gather_sent(2, b1s, b1r, "tm")
    scatter_sent(3, a2s, a2r)
    gather_sent(4, b2s, b2r, "tm")
    gather_sent(5, c2s, c2r, "src")
    scatter_sent(6, a3s, a3r)
    gather_sent(7, b3s, b3r, "tm")
    gather_sent(8, c3s, c3r, "src")


def body(ns, nt, *arrays):
    *arrays, attitude, calibration = arrays
    vmem = pl.BlockSpec(memory_space=pltpu.VMEM)
    shard = SHARD + 1
    iteration = [
        pltpu.VMEM((ns, shard, LANES), F32),
        pltpu.VMEM((ns, shard, LANES), F32),
        pltpu.VMEM((shard, LANES), F32),
        pltpu.VMEM((nt, shard, LANES), F32),
        pltpu.VMEM((shard, LANES), F32),
        pltpu.VMEM((ns, shard, LANES), F32),
    ]
    params, att, cal, resid = pl.pallas_call(
        functools.partial(kernel, ns, nt),
        out_shape=(
            jax.ShapeDtypeStruct((5, SRC), F32),
            jax.ShapeDtypeStruct((1, LANES), F32),
            jax.ShapeDtypeStruct((256, LANES), F32),
            jax.ShapeDtypeStruct((ROWS, SLOT), F32),
        ),
        in_specs=[vmem] * 11,
        out_specs=(vmem,) * 4,
        scratch_shapes=[
            pltpu.VMEM((13, ROWS, SLOT), F32),
            pltpu.VMEM((ROWS, 256, SLOT), BF16),
            pltpu.VMEM((256, OBS), BF16),
            pltpu.VMEM((SRC, OBS), BF16),
            pltpu.VMEM((256, OBS), BF16),
            pltpu.VMEM((32, OBS), BF16),
            pltpu.VMEM((128, 128), F32),
            pltpu.VMEM((16, LANES), F32),
            pltpu.VMEM((8, LANES), F32),
            pltpu.VMEM((nt, 1, LANES), F32),
            pltpu.VMEM((1, LANES), F32),
            pltpu.VMEM((ns, 16, LANES), F32),
            pltpu.VMEM((ns, 16, LANES), F32),
            pltpu.VMEM((16, LANES), F32),
            pltpu.VMEM((nt, 16, LANES), F32),
            pltpu.VMEM((2, 8, LANES), F32),
            *iteration,
            *iteration,
            pltpu.SemaphoreType.DMA((10, ns)),
            pltpu.SemaphoreType.DMA((10, ns)),
        ],
        compiler_params=pltpu.CompilerParams(
            collective_id=0, has_side_effects=True, vmem_limit_bytes=40 * 2**20
        ),
        name="astrometric",
    )(*arrays, attitude.reshape(1, LANES), calibration.reshape(256, LANES))
    return params, att.reshape(LANES), cal.reshape(-1), resid


def solution(mesh):
    spread = P(None, ("src", "tm"))
    return jax.shard_map(
        functools.partial(body, mesh.shape["src"], mesh.shape["tm"]),
        mesh=mesh,
        in_specs=(
            spread,
            spread,
            spread,
            P(None, None, ("src", "tm")),
            P(None, None, ("src", "tm")),
            spread,
            spread,
            spread,
            spread,
            P("tm"),
            P(),
        ),
        out_specs=(spread, P("tm"), P(), spread),
        check_vma=False,
    )
```

```python
import functools

import jax
import jax.numpy as jnp
from jax import lax
from jax.experimental import pallas as pl
from jax.experimental.pallas import tpu as pltpu
from jax.sharding import PartitionSpec as P

MESH = pl.DeviceIdType.MESH
F32, BF16 = jnp.float32, jnp.bfloat16
ROWS, SLOT, SRC, KNOTS, LANES = 16, 256, 128, 32, 128
OBS = ROWS * SLOT
SHARD = 8
PAIRS = [(i, j) for i in range(5) for j in range(i + 1)]
TILES = [(i, h) for i in range(2) for h in range(2)]
NT = (((1,), (1,)), ((), ()))
VMEM_LIMIT = 48 * 2**20


def iota(shape, axis):
    return lax.broadcasted_iota(jnp.int32, shape, axis)


def loop(count, step, unroll=1):
    def body(at, carry):
        step(at)
        return carry

    lax.fori_loop(0, count, body, 0, unroll=unroll)


def split(value):
    head = value.astype(BF16).astype(F32)
    return head, value - head


def nt_dot(left, right):
    return lax.dot_general(left, right, NT, preferred_element_type=F32)


def whole(tiles):
    return jnp.concatenate(
        [jnp.concatenate([tiles[i, 0], tiles[i, 1]], axis=1) for i in range(2)], axis=0
    )


def tile(ref, i, h):
    return ref[8 * i : 8 * i + 8, 128 * h : 128 * h + 128]


def along(table, places):
    return jnp.take_along_axis(table, places, axis=1)


def wide(row, rows=8):
    return jnp.broadcast_to(row, (rows, row.shape[-1]))


def choose(rows, order):
    place = iota((8, rows[0].shape[-1]), 0)
    out = wide(rows[order[0]])
    for r in range(1, 8):
        if order[r] != order[r - 1]:
            out = jnp.where(place >= r, wide(rows[order[r]]), out)
    return out


def factor_of(entries):
    low, inv = {}, {}
    for i in range(5):
        for j in range(i + 1):
            rest = entries[i, j]
            for o in range(j):
                rest = rest - low[i, o] * low[j, o]
            if i == j:
                inv[i] = 1.0 / jnp.sqrt(rest)
            else:
                low[i, j] = rest * inv[j]
    return low, inv


def solve_with(low, inv, right):
    forward = []
    for i in range(5):
        rest = right[i]
        for o in range(i):
            rest = rest - low[i, o] * forward[o]
        forward.append(rest * inv[i])
    out = [None] * 5
    for i in reversed(range(5)):
        rest = forward[i]
        for o in range(i + 1, 5):
            rest = rest - low[o, i] * out[o]
        out[i] = rest * inv[i]
    return out


def by_channel(shape):
    lane = iota(shape, 1)
    return 4 * (lane % 32) + lane // 32


def by_knot(shape):
    lane = iota(shape, 1)
    return 32 * (lane % 4) + lane // 4


def band_place(shape):
    lane = iota(shape, 1)
    return iota(shape, 0) + 32 * (lane // 32) + lane % 4


UNROLL = {"design": 1, "hot": 2, "units": 2, "source": 2, "side": 2, "offsets": 2}


class Device:
    def __init__(self, ns, nt, refs):
        self.ns, self.nt = ns, nt
        self.__dict__.update(refs)

    def row(self, at, k):
        return self.rows_s[at, pl.ds(k, 1), :]

    def prepare(self):
        rows_s = self.rows_s
        weight = self.pres[...].astype(F32) * self.wobs[...]
        root = jnp.sqrt(weight)
        u = self.ph[...]
        square = u * u
        cube = square * u
        other = 1.0 - u
        basis = [
            other * other * other / 6.0,
            (3.0 * cube - 6.0 * square + 4.0) / 6.0,
            (-3.0 * cube + 3.0 * square + 3.0 * u + 1.0) / 6.0,
            cube / 6.0,
        ]
        for j in range(4):
            rows_s[j] = basis[j] * root
            rows_s[4 + j] = basis[j]
        rows_s[8] = weight
        rows_s[9] = root
        head, tail = split(weight)
        rows_s[10] = head
        rows_s[11] = tail

    def design(self, out):
        spread = band_place((ROWS, LANES))
        group = (iota((ROWS, LANES), 1) % 32) // 4
        dd, ap = self.dd, self.ap

        def build(k):
            knot = iota((KNOTS, SLOT), 0) - wide(self.kb[pl.ds(k, 1), :], KNOTS)
            share = jnp.zeros((KNOTS, SLOT), F32)
            for j in range(4):
                share = jnp.where(knot == j, wide(self.row(j, k), KNOTS), share)
            for c in range(4):
                value = share * wide(ap[c, pl.ds(k, 1), :], KNOTS)
                head, tail = split(value)
                dd[k, 32 * c : 32 * c + 32, :] = head.astype(BF16)
                dd[k, 128 + 32 * c : 160 + 32 * c, :] = tail.astype(BF16)

        def design_row(k):
            both = dd[k]
            full = nt_dot(both, both)
            build(lax.rem(k + 1, ROWS))
            normal = full[:128, :128] + full[:128, 128:] + full[128:, :128] + full[128:, 128:]
            packed = jnp.zeros((ROWS, LANES), F32)
            for g in range(8):
                part = along(normal[16 * g : 16 * g + 16], (spread + 16 * g) & 127)
                packed = jnp.where(group == g, part, packed)
            out[2 * k] = packed[:8]
            out[2 * k + 1] = packed[8:]

        build(0)
        loop(ROWS, design_row, UNROLL["design"])

    def hot(self):
        def hot_row(k):
            ids = self.cid[pl.ds(k, 1), :]
            hit = iota((256, SLOT), 0) == wide(lax.shift_right_logical(ids, 7), 256)
            self.hot_hi[:, lanes(k)] = jnp.where(hit, 1.0, 0.0).astype(BF16)
            hit = iota((SRC, SLOT), 0) == wide(self.sid[pl.ds(k, 1), :], SRC)
            self.hot_src[:, lanes(k)] = jnp.where(hit, 1.0, 0.0).astype(BF16)

        loop(ROWS, hot_row, UNROLL["hot"])

    def unit_sums(self, out):
        units = self.units

        def unit_row(k):
            low = self.cid[pl.ds(k, 1), :] & 127
            hit = iota((LANES, SLOT), 0) == wide(low, LANES)
            for at in (0, 1):
                value = jnp.where(hit, wide(self.row(10 + at, k), LANES), 0.0)
                units[128 * at : 128 * at + 128, lanes(k)] = value.astype(BF16)

        loop(ROWS, unit_row, UNROLL["units"])
        both = nt_dot(self.hot_hi[...], units[...])
        sums = both[:, :128] + both[:, 128:]
        for s in range(self.ns):
            out[s, 0:8, :] = sums[8 * s : 8 * s + 8]

    def source_normals(self):
        sp, lhs = self.sp, self.lhs

        def source_row(k):
            a = [sp[i, pl.ds(k, 1), :] for i in range(5)]
            parts = []
            for first in (0, 8):
                chosen = (PAIRS + [(4, 4)])[first : first + 8]
                left = choose(a, [p[0] for p in chosen])
                parts.append(left * choose(a, [p[1] for p in chosen]) * wide(self.row(8, k)))
            value = jnp.concatenate(parts, axis=0)
            head, tail = split(value)
            lhs[:16, lanes(k)] = head.astype(BF16)
            lhs[16:, lanes(k)] = tail.astype(BF16)

        loop(ROWS, source_row, UNROLL["source"])
        sums = nt_dot(lhs[...], self.hot_src[...])
        sums = sums[:16] + sums[16:]
        entries = {}
        for at, (i, j) in enumerate(PAIRS):
            entries[i, j] = sums[at : at + 1] + (1.0 if i == j else 0.0)
        low, inv = factor_of(entries)
        keep = [low[i, j] for i, j in PAIRS if i != j] + [inv[i] for i in range(5)]
        for at, value in enumerate(keep):
            self.fac[at : at + 1] = value

    def offsets(self, table):
        head, tail = split(table.T)
        self.cal_t[:128, :] = head.astype(BF16)
        self.cal_t[128:, :] = tail.astype(BF16)

        def offset_row(k):
            got = jnp.dot(self.cal_t[...], self.hot_hi[:, lanes(k)], preferred_element_type=F32)
            got = got[:128] + got[128:]
            hit = iota((LANES, SLOT), 0) == wide(self.cid[pl.ds(k, 1), :] & 127, LANES)
            self.rows_s[13, pl.ds(k, 1), :] = jnp.sum(
                jnp.where(hit, got, 0.0), axis=0, keepdims=True
            )

        loop(ROWS, offset_row, UNROLL["offsets"])

    def remaining(self, table):
        out = {}
        for t in TILES:
            i, h = t
            base = tile(self.kb, i, h)
            model = jnp.zeros((8, LANES), F32)
            for j in range(4):
                sum_c = jnp.zeros((8, LANES), F32)
                for c in range(4):
                    part = along(table[8 * i : 8 * i + 8], base + (32 * c + j))
                    sum_c = sum_c + tile(self.ap.at[c], i, h) * part
                model = model + tile(self.rows_s.at[4 + j], i, h) * sum_c
            out[t] = tile(self.obs, i, h) - model - tile(self.rows_s.at[13], i, h)
        return out

    def less_sources(self, target, params):
        out = {}
        for t in TILES:
            ids = tile(self.sid, *t)
            total = jnp.zeros((8, LANES), F32)
            for i in range(5):
                total = total + tile(self.sp.at[i], *t) * along(wide(params[i]), ids)
            out[t] = target[t] - total
        return out

    def solve_sources(self, target):
        sp, lhs = self.sp, self.lhs
        self.rows_s[12] = self.rows_s[8] * whole(target)

        def side_row(k):
            a = [sp[i, pl.ds(k, 1), :] for i in range(5)]
            value = choose(a, [0, 1, 2, 3, 4, 4, 4, 4]) * wide(self.row(12, k))
            head, tail = split(value)
            lhs[:16, lanes(k)] = jnp.concatenate([head, tail], axis=0).astype(BF16)

        loop(ROWS, side_row, UNROLL["side"])
        sums = nt_dot(lhs[:16, :], self.hot_src[...])
        sums = sums[:8] + sums[8:]
        kept = [self.fac[at : at + 1] for at in range(15)]
        low = dict(zip([p for p in PAIRS if p[0] != p[1]], kept[:10]))
        return solve_with(low, kept[10:], [sums[i : i + 1] for i in range(5)])

    def right_sides(self, resid, out):
        resid = whole(resid)
        head, tail = split(self.rows_s[8] * resid)
        self.rows_s[10] = head
        self.rows_s[11] = tail
        self.unit_sums(out)
        self.attitude_sides(resid, out)

    def attitude_sides(self, resid, out):
        head, tail = split(self.rows_s[9] * resid)
        left = jnp.concatenate([head, tail], axis=0).astype(BF16)
        for k in range(ROWS):
            got = nt_dot(left, self.dd[k])
            got = got[:, :128] + got[:, 128:]
            got = got[k : k + 1] + got[16 + k : 17 + k]
            out[2 * k, 8:9, :] = got
            out[2 * k + 1, 8:9, :] = got

    def unpack(self, packed):
        lane = iota((ROWS, LANES), 1)
        rows = []
        for g in range(8):
            index = iota((ROWS, LANES), 0) + 16 * g
            ahead = (lane - index) & 127
            place = 32 * (ahead // 32) + 4 * g + ahead % 4
            rows.append(jnp.where(ahead % 32 < 4, along(packed, place), 0.0))
        upper = jnp.concatenate(rows, axis=0)
        r_id, c_id = iota((LANES, LANES), 0), iota((LANES, LANES), 1)
        strict = jnp.where(r_id % 32 == c_id % 32, 0.0, upper)
        full = upper + strict.T + jnp.where(r_id == c_id, 1.0, 0.0)
        order = by_knot((LANES, LANES))
        self.matrix[...] = along(along(full, order).T, order)

    def invert(self, blocks):
        matrix = self.matrix
        lane = iota((ROWS, LANES), 1)
        low = iota((ROWS, LANES), 0)
        lines = {s: matrix[16 * s : 16 * s + 16, :] for s in blocks}
        for j in range(ROWS):
            for s in blocks:
                i = 16 * s + j
                line = lines[s]
                column = along(line, jnp.full((ROWS, LANES), i, jnp.int32))
                pivot = 1.0 / wide(column[j : j + 1])
                scaled = jnp.where(lane[:8] == i, pivot, wide(line[j : j + 1]) * pivot)
                scaled = jnp.concatenate([scaled, scaled], axis=0)
                rest = jnp.where(lane == i, 0.0, line) - column * scaled
                lines[s] = jnp.where(low == j, scaled, rest)
        zeros = jnp.zeros((ROWS, LANES), F32)
        inner = jnp.concatenate([lines.get(s, zeros) for s in range(8)], axis=0)
        moved = jnp.dot(
            matrix[...], inner, precision=lax.Precision.HIGHEST, preferred_element_type=F32
        )
        kept = jnp.ones((ROWS, LANES), F32)
        for s in blocks:
            kept = jnp.where(lane // 16 == s, 0.0, kept)
        for s in range(8):
            rows = slice(16 * s, 16 * s + 16)
            if s in blocks:
                matrix[rows, :] = lines[s]
            else:
                matrix[rows, :] = matrix[rows, :] * kept - moved[rows]

    def advance(self, got, later, offsets, q):
        later[0:8, :] = offsets + got[0:8] * self.inv_den[...]
        step = jnp.dot(
            along(wide(got[8:9]), by_knot((8, LANES))),
            self.matrix[...],
            precision=lax.Precision.HIGHEST,
            preferred_element_type=F32,
        )
        later[8:9, :] = q + along(step, by_channel((8, LANES)))[0:1]


INPUTS = ["obs", "wobs", "pres", "sp", "ap", "ph", "kb", "sid", "cid", "att", "cal"]
OUTPUTS = ["params_o", "att_o", "cal_o", "res_o"]


def shapes(ns, nt):
    shard = SHARD + 1
    vmem = lambda *shape: pltpu.VMEM(shape, F32)
    out = {
        "rows_s": vmem(14, ROWS, SLOT),
        "dd": pltpu.VMEM((ROWS, 256, SLOT), BF16),
        "hot_hi": pltpu.VMEM((256, OBS), BF16),
        "hot_src": pltpu.VMEM((SRC, OBS), BF16),
        "units": pltpu.VMEM((256, OBS), BF16),
        "lhs": pltpu.VMEM((32, OBS), BF16),
        "cal_t": pltpu.VMEM((256, 256), BF16),
        "matrix": vmem(LANES, LANES),
        "fac": vmem(16, LANES),
        "inv_den": vmem(8, LANES),
        "qbuf": vmem(nt, 1, LANES),
        "qsend": vmem(1, LANES),
        "ns_s": vmem(ns, 8, LANES),
        "ns_r": vmem(ns, 8, LANES),
        "nt_s": vmem(8, LANES),
        "nt_r": vmem(nt, 8, LANES),
        "ws_s": vmem(ns, 8, LANES),
        "ws_r": vmem(ns, 8, LANES),
        "wt_s": vmem(8, LANES),
        "wt_r": vmem(nt, 8, LANES),
        "pair_r": vmem(2, 8, LANES),
    }
    for n in (2, 3):
        out[f"a{n}s"] = vmem(ns, shard, LANES)
        out[f"a{n}r"] = vmem(ns, shard, LANES)
        out[f"b{n}s"] = vmem(shard, LANES)
        out[f"b{n}r"] = vmem(nt, shard, LANES)
        out[f"c{n}s"] = vmem(shard, LANES)
        out[f"c{n}r"] = vmem(ns, shard, LANES)
    return out


def lanes(k):
    return pl.ds(pl.multiple_of(k * SLOT, SLOT), SLOT)


def ring_order(count):
    return sorted(range(1, count), key=lambda o: -min(o, count - o))


def plane_order(ns):
    far = (0, 1, 2, 1)
    every = [(y, x, c) for y in range(4) for x in range(4) for c in range(ns // 16)]
    return sorted(every, key=lambda o: -4 * (far[o[0]] + far[o[1]]) - o[2])[:-1]


def kernel(ns, nt, *refs):
    count = len(INPUTS)
    given = dict(zip(INPUTS, refs[:count]))
    results = dict(zip(OUTPUTS, refs[count : count + 4]))
    scratch = refs[count + 4 :]
    names = list(shapes(ns, nt))
    d = Device(ns, nt, dict(zip(names, scratch)))
    local = dict(zip(INPUTS, scratch[len(names) : len(names) + count]))
    d.__dict__.update(local)
    send, recv, load = scratch[len(names) + count :]
    me_s, me_t = lax.axis_index("src"), lax.axis_index("tm")
    my_y, my_x, my_c = me_s // 8, lax.rem(me_s // 2, 4), lax.rem(me_s, 2)

    def fetch(name):
        at = INPUTS.index(name)
        return pltpu.make_async_copy(given[name], local[name], load.at[at])

    def ready(*wanted):
        for name in wanted:
            fetch(name).wait()

    in_plane = [
        lax.rem(my_y + y, 4) * 8 + lax.rem(my_x + x, 4) * 2 + lax.rem(my_c + c, 2)
        for y, x, c in plane_order(ns)
    ]
    in_ring = [lax.rem(me_t + o, nt) for o in ring_order(nt)]

    def partners(axis, step):
        for other in in_plane if axis == "src" else in_ring:
            step(other)

    def partners_loop(axis, step):
        size, me = (ns, me_s) if axis == "src" else (nt, me_t)
        loop(size - 1, lambda at: step(lax.rem(me + 1 + at, size)))

    class Exchange:
        def __init__(self, stage, axis, source, target, shards=False):
            self.stage, self.axis, self.source, self.target = stage, axis, source, target
            self.me = me_s if axis == "src" else me_t
            self.shards = shards

        def copy(self, other, slot, sender):
            return pltpu.make_async_remote_copy(
                src_ref=self.source.at[other] if self.shards else self.source,
                dst_ref=self.target.at[slot],
                send_sem=send.at[self.stage, other],
                recv_sem=recv.at[self.stage, sender],
                device_id=(other, me_t) if self.axis == "src" else (me_s, other),
                device_id_type=MESH,
            )

        def start(self):
            partners(self.axis, lambda o: self.copy(o, self.me, self.me).start())
            self.target[self.me] = self.source[self.me] if self.shards else self.source[...]

        def wait(self):
            partners_loop(self.axis, lambda o: self.copy(o, o, o).wait_recv())

        def sent(self):
            partners_loop(self.axis, lambda o: self.copy(o, self.me, self.me).wait_send())

        def total(self):
            return jnp.sum(self.target[...], axis=0)

    barrier = pltpu.get_barrier_semaphore()

    def greet_src(o):
        pl.semaphore_signal(barrier, inc=1, device_id=(o, me_t), device_id_type=MESH)

    def greet_tm(o):
        pl.semaphore_signal(barrier, inc=1, device_id=(me_s, o), device_id_type=MESH)

    partners("tm", greet_tm)
    for name in ("wobs", "pres", "ph", "kb", "ap", "att", "cid", "sid", "sp", "cal", "obs"):
        fetch(name).start()
    partners("src", greet_src)

    first_q = Exchange(0, "tm", d.qsend, d.qbuf)
    normals_s = Exchange(1, "src", d.ns_s, d.ns_r, shards=True)
    normals_t = Exchange(2, "tm", d.nt_s, d.nt_r)
    weights_s = Exchange(3, "src", d.ws_s, d.ws_r, shards=True)
    weights_t = Exchange(4, "tm", d.wt_s, d.wt_r)

    ready("wobs", "pres", "ph")
    d.prepare()
    ready("kb", "ap")
    d.design(d.ns_s)
    ready("att")
    d.qsend[...] = along(wide(d.att[...]), by_channel((8, LANES)))[0:1]

    pl.semaphore_wait(barrier, ns + nt - 2)
    first_q.start()
    normals_s.start()
    ready("cid", "sid")
    d.hot()
    d.unit_sums(d.ws_s)
    weights_s.start()
    ready("sp")
    d.source_normals()
    ready("cal", "obs")
    d.offsets(d.cal[...])
    normals_s.wait()
    d.nt_s[...] = normals_s.total()
    normals_t.start()
    weights_s.wait()
    d.wt_s[...] = weights_s.total()
    weights_t.start()

    def reduce(n):
        at = 5 + 3 * (n - 2)
        return (
            Exchange(at, "src", getattr(d, f"a{n}s"), getattr(d, f"a{n}r"), shards=True),
            Exchange(at + 1, "tm", getattr(d, f"b{n}s"), getattr(d, f"b{n}r")),
            Exchange(at + 2, "src", getattr(d, f"c{n}s"), getattr(d, f"c{n}r")),
        )

    over_src, over_tm, back = reduce(2)
    first_q.wait()
    table = jnp.concatenate([d.qbuf[k] for k in range(nt)], axis=0)
    target = d.remaining(table)
    params = d.solve_sources(target)
    d.right_sides(d.less_sources(target, params), d.a2s)
    over_src.start()

    normals_t.wait()
    half = my_c
    owned = me_s // 2
    d.pair_r[half] = normals_t.total()
    swap = pltpu.make_async_remote_copy(
        src_ref=d.pair_r.at[half],
        dst_ref=d.pair_r.at[half],
        send_sem=send.at[11, 0],
        recv_sem=recv.at[11, 0],
        device_id=(me_s + 1 - 2 * half, me_t),
        device_id_type=MESH,
    )
    swap.start()
    first_q.sent()
    normals_s.sent()
    swap.wait()
    d.unpack(jnp.concatenate([d.pair_r[0], d.pair_r[1]], axis=0))
    d.invert((1, 3, 5, 7))

    over_src.wait()
    d.b2s[...] = over_src.total()
    over_tm.start()
    d.invert((2, 6))
    d.invert((4,))
    d.invert((0,))
    weights_t.wait()
    d.inv_den[...] = 1.0 / (1.0 + weights_t.total())
    weights_s.sent()
    normals_t.sent()
    weights_t.sent()
    over_src.sent()

    own_cal = pl.ds(pl.multiple_of(8 * me_s, 8), 8)
    over_tm.wait()
    d.advance(over_tm.total(), d.c2s, d.cal[own_cal, :], d.qbuf[owned])
    back.start()
    over_tm.sent()
    back.wait()

    def tables_of(got):
        knots = jnp.concatenate([got[2 * k, 8:9, :] for k in range(nt)], axis=0)
        return knots, got[:, 0:8, :].reshape(ns * 8, LANES)

    table, cal = tables_of(d.c2r)
    d.offsets(cal)
    target = d.remaining(table)
    params = d.solve_sources(target)
    d.right_sides(d.less_sources(target, params), d.a3s)
    back.sent()
    over_src, over_tm, back = reduce(3)
    over_src.start()
    for i in range(5):
        results["params_o"][i : i + 1, :] = params[i]
    over_src.wait()
    d.b3s[...] = over_src.total()
    over_tm.start()
    over_src.sent()
    over_tm.wait()
    d.advance(over_tm.total(), d.c3s, d.c2s[0:8, :], d.c2s[8:9, :])
    back.start()
    over_tm.sent()
    back.wait()

    table, cal = tables_of(d.c3r)
    results["cal_o"][...] = cal
    d.offsets(cal)
    results["res_o"][...] = whole(d.less_sources(d.remaining(table), params))
    results["att_o"][...] = along(wide(d.c3r[2 * me_t, 8:9, :]), by_knot((8, LANES)))[0:1]
    back.sent()


def body(ns, nt, *arrays):
    *arrays, attitude, calibration = arrays
    arrays = [*arrays, attitude.reshape(1, LANES), calibration.reshape(256, LANES)]
    arrays = [pltpu.with_memory_space_constraint(x, pltpu.HBM) for x in arrays]
    vmem = pl.BlockSpec(memory_space=pltpu.VMEM)
    params, att, cal, resid = pl.pallas_call(
        functools.partial(kernel, ns, nt),
        out_shape=(
            jax.ShapeDtypeStruct((5, SRC), F32),
            jax.ShapeDtypeStruct((1, LANES), F32),
            jax.ShapeDtypeStruct((256, LANES), F32),
            jax.ShapeDtypeStruct((ROWS, SLOT), F32),
        ),
        in_specs=[pl.BlockSpec(memory_space=pltpu.HBM)] * len(arrays),
        out_specs=(vmem,) * 4,
        scratch_shapes=[
            *shapes(ns, nt).values(),
            *(pltpu.VMEM(x.shape, x.dtype) for x in arrays),
            pltpu.SemaphoreType.DMA((12, ns)),
            pltpu.SemaphoreType.DMA((12, ns)),
            pltpu.SemaphoreType.DMA((len(arrays),)),
        ],
        compiler_params=pltpu.CompilerParams(
            collective_id=0, has_side_effects=True, vmem_limit_bytes=VMEM_LIMIT
        ),
        name="astrometric",
    )(*arrays)
    return params, att.reshape(LANES), cal.reshape(-1), resid


def solution(mesh):
    spread = P(None, ("src", "tm"))
    return jax.shard_map(
        functools.partial(body, mesh.shape["src"], mesh.shape["tm"]),
        mesh=mesh,
        in_specs=(
            spread,
            spread,
            spread,
            P(None, None, ("src", "tm")),
            P(None, None, ("src", "tm")),
            spread,
            spread,
            spread,
            spread,
            P("tm"),
            P(),
        ),
        out_specs=(spread, P("tm"), P(), spread),
        check_vma=False,
    )
```

```python
import functools

import jax
import jax.numpy as jnp
from jax import lax
from jax.experimental import pallas as pl
from jax.experimental.pallas import tpu as pltpu
from jax.sharding import PartitionSpec as P

MESH = pl.DeviceIdType.MESH
F32, BF16 = jnp.float32, jnp.bfloat16
ROWS, SLOT, SRC, KNOTS, LANES = 16, 256, 128, 32, 128
OBS = ROWS * SLOT
SHARD = 8
PAIRS = [(i, j) for i in range(5) for j in range(i + 1)]
TILES = [(i, h) for i in range(2) for h in range(2)]
NT = (((1,), (1,)), ((), ()))
VMEM_LIMIT = 48 * 2**20


def iota(shape, axis):
    return lax.broadcasted_iota(jnp.int32, shape, axis)


def loop(count, step, unroll=1):
    def body(at, carry):
        step(at)
        return carry

    lax.fori_loop(0, count, body, 0, unroll=unroll)


def split(value):
    head = value.astype(BF16).astype(F32)
    return head, value - head


def nt_dot(left, right):
    return lax.dot_general(left, right, NT, preferred_element_type=F32)


def whole(tiles):
    return jnp.concatenate(
        [jnp.concatenate([tiles[i, 0], tiles[i, 1]], axis=1) for i in range(2)], axis=0
    )


def tile(ref, i, h):
    return ref[8 * i : 8 * i + 8, 128 * h : 128 * h + 128]


def along(table, places):
    return jnp.take_along_axis(table, places, axis=1)


def wide(row, rows=8):
    return jnp.broadcast_to(row, (rows, row.shape[-1]))


def choose(rows, order):
    place = iota((8, rows[0].shape[-1]), 0)
    out = wide(rows[order[0]])
    for r in range(1, 8):
        if order[r] != order[r - 1]:
            out = jnp.where(place >= r, wide(rows[order[r]]), out)
    return out


def factor_of(entries):
    low, inv = {}, {}
    for i in range(5):
        for j in range(i + 1):
            rest = entries[i, j]
            for o in range(j):
                rest = rest - low[i, o] * low[j, o]
            if i == j:
                inv[i] = 1.0 / jnp.sqrt(rest)
            else:
                low[i, j] = rest * inv[j]
    return low, inv


def solve_with(low, inv, right):
    forward = []
    for i in range(5):
        rest = right[i]
        for o in range(i):
            rest = rest - low[i, o] * forward[o]
        forward.append(rest * inv[i])
    out = [None] * 5
    for i in reversed(range(5)):
        rest = forward[i]
        for o in range(i + 1, 5):
            rest = rest - low[o, i] * out[o]
        out[i] = rest * inv[i]
    return out


def by_channel(shape):
    lane = iota(shape, 1)
    return 4 * (lane % 32) + lane // 32


def by_knot(shape):
    lane = iota(shape, 1)
    return 32 * (lane % 4) + lane // 4


def band_place(shape):
    lane = iota(shape, 1)
    return iota(shape, 0) + 32 * (lane // 32) + lane % 4


UNROLL = {"design": 16, "hot": 16, "units": 16, "source": 16, "side": 16, "offsets": 16}


class Device:
    def __init__(self, ns, nt, refs):
        self.ns, self.nt = ns, nt
        self.__dict__.update(refs)

    def row(self, at, k):
        return self.rows_s[at, pl.ds(k, 1), :]

    def prepare(self):
        rows_s = self.rows_s
        weight = self.pres[...].astype(F32) * self.wobs[...]
        root = jnp.sqrt(weight)
        u = self.ph[...]
        square = u * u
        cube = square * u
        other = 1.0 - u
        basis = [
            other * other * other / 6.0,
            (3.0 * cube - 6.0 * square + 4.0) / 6.0,
            (-3.0 * cube + 3.0 * square + 3.0 * u + 1.0) / 6.0,
            cube / 6.0,
        ]
        for j in range(4):
            rows_s[j] = basis[j] * root
            rows_s[4 + j] = basis[j]
        rows_s[8] = weight
        rows_s[9] = root
        head, tail = split(weight)
        rows_s[10] = head
        rows_s[11] = tail

    def design(self, out):
        spread = band_place((ROWS, LANES))
        group = (iota((ROWS, LANES), 1) % 32) // 4
        dd, ap = self.dd, self.ap

        def build(k):
            knot = iota((KNOTS, SLOT), 0) - wide(self.kb[pl.ds(k, 1), :], KNOTS)
            share = jnp.zeros((KNOTS, SLOT), F32)
            for j in range(4):
                share = jnp.where(knot == j, wide(self.row(j, k), KNOTS), share)
            for c in range(4):
                value = share * wide(ap[c, pl.ds(k, 1), :], KNOTS)
                head, tail = split(value)
                dd[k, 32 * c : 32 * c + 32, :] = head.astype(BF16)
                dd[k, 128 + 32 * c : 160 + 32 * c, :] = tail.astype(BF16)

        def design_row(k):
            both = dd[k]
            full = nt_dot(both, both)
            build(lax.rem(k + 1, ROWS))
            normal = full[:128, :128] + full[:128, 128:] + full[128:, :128] + full[128:, 128:]
            packed = jnp.zeros((ROWS, LANES), F32)
            for g in range(8):
                part = along(normal[16 * g : 16 * g + 16], (spread + 16 * g) & 127)
                packed = jnp.where(group == g, part, packed)
            out[2 * k] = packed[:8]
            out[2 * k + 1] = packed[8:]

        build(0)
        loop(ROWS, design_row, UNROLL["design"])

    def hot(self):
        def hot_row(k):
            ids = self.cid[pl.ds(k, 1), :]
            hit = iota((256, SLOT), 0) == wide(lax.shift_right_logical(ids, 7), 256)
            self.hot_hi[:, lanes(k)] = jnp.where(hit, 1.0, 0.0).astype(BF16)
            hit = iota((SRC, SLOT), 0) == wide(self.sid[pl.ds(k, 1), :], SRC)
            self.hot_src[:, lanes(k)] = jnp.where(hit, 1.0, 0.0).astype(BF16)

        loop(ROWS, hot_row, UNROLL["hot"])

    def unit_sums(self, out):
        units = self.units

        def unit_row(k):
            low = self.cid[pl.ds(k, 1), :] & 127
            hit = iota((LANES, SLOT), 0) == wide(low, LANES)
            for at in (0, 1):
                value = jnp.where(hit, wide(self.row(10 + at, k), LANES), 0.0)
                units[128 * at : 128 * at + 128, lanes(k)] = value.astype(BF16)

        loop(ROWS, unit_row, UNROLL["units"])
        both = nt_dot(self.hot_hi[...], units[...])
        sums = both[:, :128] + both[:, 128:]
        for s in range(self.ns):
            out[s, 0:8, :] = sums[8 * s : 8 * s + 8]

    def source_normals(self):
        sp, lhs = self.sp, self.lhs

        def source_row(k):
            a = [sp[i, pl.ds(k, 1), :] for i in range(5)]
            parts = []
            for first in (0, 8):
                chosen = (PAIRS + [(4, 4)])[first : first + 8]
                left = choose(a, [p[0] for p in chosen])
                parts.append(left * choose(a, [p[1] for p in chosen]) * wide(self.row(8, k)))
            value = jnp.concatenate(parts, axis=0)
            head, tail = split(value)
            lhs[:16, lanes(k)] = head.astype(BF16)
            lhs[16:, lanes(k)] = tail.astype(BF16)

        loop(ROWS, source_row, UNROLL["source"])
        sums = nt_dot(lhs[...], self.hot_src[...])
        sums = sums[:16] + sums[16:]
        entries = {}
        for at, (i, j) in enumerate(PAIRS):
            entries[i, j] = sums[at : at + 1] + (1.0 if i == j else 0.0)
        low, inv = factor_of(entries)
        keep = [low[i, j] for i, j in PAIRS if i != j] + [inv[i] for i in range(5)]
        for at, value in enumerate(keep):
            self.fac[at : at + 1] = value

    def offsets(self, table):
        head, tail = split(table.T)
        self.cal_t[:128, :] = head.astype(BF16)
        self.cal_t[128:, :] = tail.astype(BF16)

        def offset_row(k):
            got = jnp.dot(self.cal_t[...], self.hot_hi[:, lanes(k)], preferred_element_type=F32)
            got = got[:128] + got[128:]
            hit = iota((LANES, SLOT), 0) == wide(self.cid[pl.ds(k, 1), :] & 127, LANES)
            self.rows_s[13, pl.ds(k, 1), :] = jnp.sum(
                jnp.where(hit, got, 0.0), axis=0, keepdims=True
            )

        loop(ROWS, offset_row, UNROLL["offsets"])

    def remaining(self, table):
        out = {}
        for t in TILES:
            i, h = t
            base = tile(self.kb, i, h)
            model = jnp.zeros((8, LANES), F32)
            for j in range(4):
                sum_c = jnp.zeros((8, LANES), F32)
                for c in range(4):
                    part = along(table[8 * i : 8 * i + 8], base + (32 * c + j))
                    sum_c = sum_c + tile(self.ap.at[c], i, h) * part
                model = model + tile(self.rows_s.at[4 + j], i, h) * sum_c
            out[t] = tile(self.obs, i, h) - model - tile(self.rows_s.at[13], i, h)
        return out

    def less_sources(self, target, params):
        out = {}
        for t in TILES:
            ids = tile(self.sid, *t)
            total = jnp.zeros((8, LANES), F32)
            for i in range(5):
                total = total + tile(self.sp.at[i], *t) * along(wide(params[i]), ids)
            out[t] = target[t] - total
        return out

    def solve_sources(self, target):
        sp, lhs = self.sp, self.lhs
        self.rows_s[12] = self.rows_s[8] * whole(target)

        def side_row(k):
            a = [sp[i, pl.ds(k, 1), :] for i in range(5)]
            value = choose(a, [0, 1, 2, 3, 4, 4, 4, 4]) * wide(self.row(12, k))
            head, tail = split(value)
            lhs[:16, lanes(k)] = jnp.concatenate([head, tail], axis=0).astype(BF16)

        loop(ROWS, side_row, UNROLL["side"])
        sums = nt_dot(lhs[:16, :], self.hot_src[...])
        sums = sums[:8] + sums[8:]
        kept = [self.fac[at : at + 1] for at in range(15)]
        low = dict(zip([p for p in PAIRS if p[0] != p[1]], kept[:10]))
        return solve_with(low, kept[10:], [sums[i : i + 1] for i in range(5)])

    def right_sides(self, resid, out):
        resid = whole(resid)
        head, tail = split(self.rows_s[8] * resid)
        self.rows_s[10] = head
        self.rows_s[11] = tail
        self.unit_sums(out)
        self.attitude_sides(resid, out)

    def attitude_sides(self, resid, out):
        head, tail = split(self.rows_s[9] * resid)
        left = jnp.concatenate([head, tail], axis=0).astype(BF16)
        for k in range(ROWS):
            got = nt_dot(left, self.dd[k])
            got = got[:, :128] + got[:, 128:]
            got = got[k : k + 1] + got[16 + k : 17 + k]
            out[2 * k, 8:9, :] = got
            out[2 * k + 1, 8:9, :] = got

    def unpack(self, packed):
        lane = iota((ROWS, LANES), 1)
        rows = []
        for g in range(8):
            index = iota((ROWS, LANES), 0) + 16 * g
            ahead = (lane - index) & 127
            place = 32 * (ahead // 32) + 4 * g + ahead % 4
            rows.append(jnp.where(ahead % 32 < 4, along(packed, place), 0.0))
        upper = jnp.concatenate(rows, axis=0)
        r_id, c_id = iota((LANES, LANES), 0), iota((LANES, LANES), 1)
        strict = jnp.where(r_id % 32 == c_id % 32, 0.0, upper)
        full = upper + strict.T + jnp.where(r_id == c_id, 1.0, 0.0)
        order = by_knot((LANES, LANES))
        self.matrix[...] = along(along(full, order).T, order)

    def invert(self, blocks):
        matrix = self.matrix
        lane = iota((ROWS, LANES), 1)
        low = iota((ROWS, LANES), 0)
        lines = {s: matrix[16 * s : 16 * s + 16, :] for s in blocks}
        for j in range(ROWS):
            for s in blocks:
                i = 16 * s + j
                line = lines[s]
                column = along(line, jnp.full((ROWS, LANES), i, jnp.int32))
                pivot = 1.0 / wide(column[j : j + 1])
                scaled = jnp.where(lane[:8] == i, pivot, wide(line[j : j + 1]) * pivot)
                scaled = jnp.concatenate([scaled, scaled], axis=0)
                rest = jnp.where(lane == i, 0.0, line) - column * scaled
                lines[s] = jnp.where(low == j, scaled, rest)
        zeros = jnp.zeros((ROWS, LANES), F32)
        inner = jnp.concatenate([lines.get(s, zeros) for s in range(8)], axis=0)
        moved = jnp.dot(
            matrix[...], inner, precision=lax.Precision.HIGHEST, preferred_element_type=F32
        )
        kept = jnp.ones((ROWS, LANES), F32)
        for s in blocks:
            kept = jnp.where(lane // 16 == s, 0.0, kept)
        for s in range(8):
            rows = slice(16 * s, 16 * s + 16)
            if s in blocks:
                matrix[rows, :] = lines[s]
            else:
                matrix[rows, :] = matrix[rows, :] * kept - moved[rows]

    def advance(self, got, later, offsets, q):
        later[0:8, :] = offsets + got[0:8] * self.inv_den[...]
        step = jnp.dot(
            along(wide(got[8:9]), by_knot((8, LANES))),
            self.matrix[...],
            precision=lax.Precision.HIGHEST,
            preferred_element_type=F32,
        )
        later[8:9, :] = q + along(step, by_channel((8, LANES)))[0:1]


INPUTS = ["obs", "wobs", "pres", "sp", "ap", "ph", "kb", "sid", "cid", "att", "cal"]
OUTPUTS = ["params_o", "att_o", "cal_o", "res_o"]


def shapes(ns, nt):
    shard = SHARD + 1
    vmem = lambda *shape: pltpu.VMEM(shape, F32)
    out = {
        "rows_s": vmem(14, ROWS, SLOT),
        "dd": pltpu.VMEM((ROWS, 256, SLOT), BF16),
        "hot_hi": pltpu.VMEM((256, OBS), BF16),
        "hot_src": pltpu.VMEM((SRC, OBS), BF16),
        "units": pltpu.VMEM((256, OBS), BF16),
        "lhs": pltpu.VMEM((32, OBS), BF16),
        "cal_t": pltpu.VMEM((256, 256), BF16),
        "matrix": vmem(LANES, LANES),
        "fac": vmem(16, LANES),
        "inv_den": vmem(8, LANES),
        "qbuf": vmem(nt, 1, LANES),
        "qsend": vmem(1, LANES),
        "ns_s": vmem(ns, 8, LANES),
        "ns_r": vmem(ns, 8, LANES),
        "nt_s": vmem(8, LANES),
        "nt_r": vmem(nt, 8, LANES),
        "ws_s": vmem(ns, 8, LANES),
        "ws_r": vmem(ns, 8, LANES),
        "wt_s": vmem(8, LANES),
        "wt_r": vmem(nt, 8, LANES),
        "pair_r": vmem(2, 8, LANES),
    }
    for n in (2, 3):
        out[f"a{n}s"] = vmem(ns, shard, LANES)
        out[f"a{n}r"] = vmem(ns, shard, LANES)
        out[f"b{n}s"] = vmem(shard, LANES)
        out[f"b{n}r"] = vmem(nt, shard, LANES)
        out[f"c{n}s"] = vmem(shard, LANES)
        out[f"c{n}r"] = vmem(ns, shard, LANES)
    return out


def lanes(k):
    return pl.ds(pl.multiple_of(k * SLOT, SLOT), SLOT)


def ring_order(count):
    return sorted(range(1, count), key=lambda o: -min(o, count - o))


def plane_order(ns):
    far = (0, 1, 2, 1)
    every = [(y, x, c) for y in range(4) for x in range(4) for c in range(ns // 16)]
    return sorted(every, key=lambda o: -4 * (far[o[0]] + far[o[1]]) - o[2])[:-1]


def kernel(ns, nt, *refs):
    count = len(INPUTS)
    given = dict(zip(INPUTS, refs[:count]))
    results = dict(zip(OUTPUTS, refs[count : count + 4]))
    scratch = refs[count + 4 :]
    names = list(shapes(ns, nt))
    d = Device(ns, nt, dict(zip(names, scratch)))
    local = dict(zip(INPUTS, scratch[len(names) : len(names) + count]))
    d.__dict__.update(local)
    send, recv, load = scratch[len(names) + count :]
    me_s, me_t = lax.axis_index("src"), lax.axis_index("tm")
    my_y, my_x, my_c = me_s // 8, lax.rem(me_s // 2, 4), lax.rem(me_s, 2)

    def fetch(name):
        at = INPUTS.index(name)
        return pltpu.make_async_copy(given[name], local[name], load.at[at])

    def ready(*wanted):
        for name in wanted:
            fetch(name).wait()

    in_plane = [
        lax.rem(my_y + y, 4) * 8 + lax.rem(my_x + x, 4) * 2 + lax.rem(my_c + c, 2)
        for y, x, c in plane_order(ns)
    ]
    in_ring = [lax.rem(me_t + o, nt) for o in ring_order(nt)]

    def partners(axis, step):
        for other in in_plane if axis == "src" else in_ring:
            step(other)

    def partners_loop(axis, step):
        size, me = (ns, me_s) if axis == "src" else (nt, me_t)
        loop(size - 1, lambda at: step(lax.rem(me + 1 + at, size)))

    class Exchange:
        def __init__(self, stage, axis, source, target, shards=False):
            self.stage, self.axis, self.source, self.target = stage, axis, source, target
            self.me = me_s if axis == "src" else me_t
            self.shards = shards

        def copy(self, other, slot, sender):
            return pltpu.make_async_remote_copy(
                src_ref=self.source.at[other] if self.shards else self.source,
                dst_ref=self.target.at[slot],
                send_sem=send.at[self.stage, other],
                recv_sem=recv.at[self.stage, sender],
                device_id=(other, me_t) if self.axis == "src" else (me_s, other),
                device_id_type=MESH,
            )

        def start(self):
            partners(self.axis, lambda o: self.copy(o, self.me, self.me).start())
            self.target[self.me] = self.source[self.me] if self.shards else self.source[...]

        def wait(self):
            partners_loop(self.axis, lambda o: self.copy(o, o, o).wait_recv())

        def sent(self):
            partners_loop(self.axis, lambda o: self.copy(o, self.me, self.me).wait_send())

        def total(self):
            return jnp.sum(self.target[...], axis=0)

    barrier = pltpu.get_barrier_semaphore()

    def greet_src(o):
        pl.semaphore_signal(barrier, inc=1, device_id=(o, me_t), device_id_type=MESH)

    def greet_tm(o):
        pl.semaphore_signal(barrier, inc=1, device_id=(me_s, o), device_id_type=MESH)

    partners("tm", greet_tm)
    for name in ("wobs", "pres", "ph", "kb", "ap", "att", "cid", "sid", "sp", "cal", "obs"):
        fetch(name).start()
    partners("src", greet_src)

    first_q = Exchange(0, "tm", d.qsend, d.qbuf)
    normals_s = Exchange(1, "src", d.ns_s, d.ns_r, shards=True)
    normals_t = Exchange(2, "tm", d.nt_s, d.nt_r)
    weights_s = Exchange(3, "src", d.ws_s, d.ws_r, shards=True)
    weights_t = Exchange(4, "tm", d.wt_s, d.wt_r)

    ready("wobs", "pres", "ph")
    d.prepare()
    ready("kb", "ap")
    d.design(d.ns_s)
    ready("att")
    d.qsend[...] = along(wide(d.att[...]), by_channel((8, LANES)))[0:1]

    pl.semaphore_wait(barrier, ns + nt - 2)
    first_q.start()
    normals_s.start()
    ready("cid", "sid")
    d.hot()
    d.unit_sums(d.ws_s)
    weights_s.start()
    ready("sp")
    d.source_normals()
    ready("cal", "obs")
    d.offsets(d.cal[...])
    normals_s.wait()
    d.nt_s[...] = normals_s.total()
    normals_t.start()
    weights_s.wait()
    d.wt_s[...] = weights_s.total()
    weights_t.start()

    def reduce(n):
        at = 5 + 3 * (n - 2)
        return (
            Exchange(at, "src", getattr(d, f"a{n}s"), getattr(d, f"a{n}r"), shards=True),
            Exchange(at + 1, "tm", getattr(d, f"b{n}s"), getattr(d, f"b{n}r")),
            Exchange(at + 2, "src", getattr(d, f"c{n}s"), getattr(d, f"c{n}r")),
        )

    over_src, over_tm, back = reduce(2)
    first_q.wait()
    table = jnp.concatenate([d.qbuf[k] for k in range(nt)], axis=0)
    target = d.remaining(table)
    params = d.solve_sources(target)
    d.right_sides(d.less_sources(target, params), d.a2s)
    over_src.start()

    normals_t.wait()
    half = my_c
    owned = me_s // 2
    d.pair_r[half] = normals_t.total()
    swap = pltpu.make_async_remote_copy(
        src_ref=d.pair_r.at[half],
        dst_ref=d.pair_r.at[half],
        send_sem=send.at[11, 0],
        recv_sem=recv.at[11, 0],
        device_id=(me_s + 1 - 2 * half, me_t),
        device_id_type=MESH,
    )
    swap.start()
    first_q.sent()
    normals_s.sent()
    swap.wait()
    d.unpack(jnp.concatenate([d.pair_r[0], d.pair_r[1]], axis=0))
    d.invert((1, 3, 5, 7))

    over_src.wait()
    d.b2s[...] = over_src.total()
    over_tm.start()
    d.invert((2, 6))
    d.invert((4,))
    d.invert((0,))
    weights_t.wait()
    d.inv_den[...] = 1.0 / (1.0 + weights_t.total())
    weights_s.sent()
    normals_t.sent()
    weights_t.sent()
    over_src.sent()

    own_cal = pl.ds(pl.multiple_of(8 * me_s, 8), 8)
    over_tm.wait()
    d.advance(over_tm.total(), d.c2s, d.cal[own_cal, :], d.qbuf[owned])
    back.start()
    over_tm.sent()
    back.wait()

    def tables_of(got):
        knots = jnp.concatenate([got[2 * k, 8:9, :] for k in range(nt)], axis=0)
        return knots, got[:, 0:8, :].reshape(ns * 8, LANES)

    table, cal = tables_of(d.c2r)
    d.offsets(cal)
    target = d.remaining(table)
    params = d.solve_sources(target)
    d.right_sides(d.less_sources(target, params), d.a3s)
    back.sent()
    over_src, over_tm, back = reduce(3)
    over_src.start()
    for i in range(5):
        results["params_o"][i : i + 1, :] = params[i]
    over_src.wait()
    d.b3s[...] = over_src.total()
    over_tm.start()
    over_src.sent()
    over_tm.wait()
    d.advance(over_tm.total(), d.c3s, d.c2s[0:8, :], d.c2s[8:9, :])
    back.start()
    over_tm.sent()
    back.wait()

    table, cal = tables_of(d.c3r)
    results["cal_o"][...] = cal
    d.offsets(cal)
    results["res_o"][...] = whole(d.less_sources(d.remaining(table), params))
    results["att_o"][...] = along(wide(d.c3r[2 * me_t, 8:9, :]), by_knot((8, LANES)))[0:1]
    back.sent()


def publish(*arrays):
    def copy(*refs):
        *refs, load = refs
        count = len(refs) // 2
        copies = [
            pltpu.make_async_copy(refs[at], refs[count + at], load.at[at]) for at in range(count)
        ]
        for each in copies:
            each.start()
        for each in copies:
            each.wait()

    return pl.pallas_call(
        copy,
        out_shape=tuple(jax.ShapeDtypeStruct(x.shape, x.dtype) for x in arrays),
        in_specs=[pl.BlockSpec(memory_space=pltpu.VMEM)] * len(arrays),
        out_specs=(pl.BlockSpec(memory_space=pltpu.HBM),) * len(arrays),
        scratch_shapes=[pltpu.SemaphoreType.DMA((len(arrays),))],
        name="publish",
    )(*arrays)


def body(ns, nt, *arrays):
    *arrays, attitude, calibration = arrays
    arrays = [*arrays, attitude.reshape(1, LANES), calibration.reshape(256, LANES)]
    arrays = [pltpu.with_memory_space_constraint(x, pltpu.HBM) for x in arrays]
    vmem = pl.BlockSpec(memory_space=pltpu.VMEM)
    params, att, cal, resid = pl.pallas_call(
        functools.partial(kernel, ns, nt),
        out_shape=(
            pltpu.VMEM((5, SRC), F32),
            pltpu.VMEM((1, LANES), F32),
            pltpu.VMEM((256, LANES), F32),
            pltpu.VMEM((ROWS, SLOT), F32),
        ),
        in_specs=[pl.BlockSpec(memory_space=pltpu.HBM)] * len(arrays),
        out_specs=(vmem,) * 4,
        scratch_shapes=[
            *shapes(ns, nt).values(),
            *(pltpu.VMEM(x.shape, x.dtype) for x in arrays),
            pltpu.SemaphoreType.DMA((12, ns)),
            pltpu.SemaphoreType.DMA((12, ns)),
            pltpu.SemaphoreType.DMA((len(arrays),)),
        ],
        compiler_params=pltpu.CompilerParams(
            collective_id=0, has_side_effects=True, vmem_limit_bytes=VMEM_LIMIT
        ),
        name="astrometric",
    )(*arrays)
    held = [pltpu.with_memory_space_constraint(x, pltpu.VMEM) for x in (params, att, cal, resid)]
    params, att, cal, resid = publish(*held)
    return params, att.reshape(LANES), cal.reshape(-1), resid


def solution(mesh):
    spread = P(None, ("src", "tm"))
    return jax.shard_map(
        functools.partial(body, mesh.shape["src"], mesh.shape["tm"]),
        mesh=mesh,
        in_specs=(
            spread,
            spread,
            spread,
            P(None, None, ("src", "tm")),
            P(None, None, ("src", "tm")),
            spread,
            spread,
            spread,
            spread,
            P("tm"),
            P(),
        ),
        out_specs=(spread, P("tm"), P(), spread),
        check_vma=False,
    )
```

```python
import functools

import jax
import jax.numpy as jnp
from jax import lax
from jax.experimental import pallas as pl
from jax.experimental.pallas import tpu as pltpu
from jax.sharding import PartitionSpec as P

MESH = pl.DeviceIdType.MESH
F32, BF16 = jnp.float32, jnp.bfloat16
ROWS, SLOT, SRC, KNOTS, LANES = 16, 256, 128, 32, 128
OBS = ROWS * SLOT
SHARD = 8
PAIRS = [(i, j) for i in range(5) for j in range(i + 1)]
TILES = [(i, h) for i in range(2) for h in range(2)]
NT = (((1,), (1,)), ((), ()))
VMEM_LIMIT = 48 * 2**20


def iota(shape, axis):
    return lax.broadcasted_iota(jnp.int32, shape, axis)


def loop(count, step, unroll=1):
    def body(at, carry):
        step(at)
        return carry

    lax.fori_loop(0, count, body, 0, unroll=unroll)


def split(value):
    head = value.astype(BF16).astype(F32)
    return head, value - head


def nt_dot(left, right):
    return lax.dot_general(left, right, NT, preferred_element_type=F32)


def whole(tiles):
    return jnp.concatenate(
        [jnp.concatenate([tiles[i, 0], tiles[i, 1]], axis=1) for i in range(2)], axis=0
    )


def tile(ref, i, h):
    return ref[8 * i : 8 * i + 8, 128 * h : 128 * h + 128]


def along(table, places):
    return jnp.take_along_axis(table, places, axis=1)


def wide(row, rows=8):
    return jnp.broadcast_to(row, (rows, row.shape[-1]))


def choose(rows, order):
    place = iota((8, rows[0].shape[-1]), 0)
    out = wide(rows[order[0]])
    for r in range(1, 8):
        if order[r] != order[r - 1]:
            out = jnp.where(place >= r, wide(rows[order[r]]), out)
    return out


def factor_of(entries):
    low, inv = {}, {}
    for i in range(5):
        for j in range(i + 1):
            rest = entries[i, j]
            for o in range(j):
                rest = rest - low[i, o] * low[j, o]
            if i == j:
                inv[i] = 1.0 / jnp.sqrt(rest)
            else:
                low[i, j] = rest * inv[j]
    return low, inv


def solve_with(low, inv, right):
    forward = []
    for i in range(5):
        rest = right[i]
        for o in range(i):
            rest = rest - low[i, o] * forward[o]
        forward.append(rest * inv[i])
    out = [None] * 5
    for i in reversed(range(5)):
        rest = forward[i]
        for o in range(i + 1, 5):
            rest = rest - low[o, i] * out[o]
        out[i] = rest * inv[i]
    return out


def by_channel(shape):
    lane = iota(shape, 1)
    return 4 * (lane % 32) + lane // 32


def by_knot(shape):
    lane = iota(shape, 1)
    return 32 * (lane % 4) + lane // 4


def band_place(shape):
    lane = iota(shape, 1)
    return iota(shape, 0) + 32 * (lane // 32) + lane % 4


UNROLL = {"design": 16, "hot": 16, "units": 16, "source": 16, "side": 16, "offsets": 16}


class Device:
    def __init__(self, ns, nt, refs):
        self.ns, self.nt = ns, nt
        self.__dict__.update(refs)

    def row(self, at, k):
        return self.rows_s[at, pl.ds(k, 1), :]

    def prepare(self):
        rows_s = self.rows_s
        weight = self.pres[...].astype(F32) * self.wobs[...]
        root = jnp.sqrt(weight)
        u = self.ph[...]
        square = u * u
        cube = square * u
        other = 1.0 - u
        basis = [
            other * other * other / 6.0,
            (3.0 * cube - 6.0 * square + 4.0) / 6.0,
            (-3.0 * cube + 3.0 * square + 3.0 * u + 1.0) / 6.0,
            cube / 6.0,
        ]
        for j in range(4):
            rows_s[j] = basis[j] * root
            rows_s[4 + j] = basis[j]
        rows_s[8] = weight
        rows_s[9] = root
        head, tail = split(weight)
        rows_s[10] = head
        rows_s[11] = tail

    def design(self, out):
        spread = band_place((ROWS, LANES))
        group = (iota((ROWS, LANES), 1) % 32) // 4
        dd, ap = self.dd, self.ap

        def build(k):
            knot = iota((KNOTS, SLOT), 0) - wide(self.kb[pl.ds(k, 1), :], KNOTS)
            share = jnp.zeros((KNOTS, SLOT), F32)
            for j in range(4):
                share = jnp.where(knot == j, wide(self.row(j, k), KNOTS), share)
            for c in range(4):
                value = share * wide(ap[c, pl.ds(k, 1), :], KNOTS)
                head, tail = split(value)
                dd[k, 32 * c : 32 * c + 32, :] = head.astype(BF16)
                dd[k, 128 + 32 * c : 160 + 32 * c, :] = tail.astype(BF16)

        def design_row(k):
            both = dd[k]
            full = nt_dot(both, both)
            build(lax.rem(k + 1, ROWS))
            normal = full[:128, :128] + full[:128, 128:] + full[128:, :128] + full[128:, 128:]
            packed = jnp.zeros((ROWS, LANES), F32)
            for g in range(8):
                part = along(normal[16 * g : 16 * g + 16], (spread + 16 * g) & 127)
                packed = jnp.where(group == g, part, packed)
            out[2 * k] = packed[:8]
            out[2 * k + 1] = packed[8:]

        build(0)
        loop(ROWS, design_row, UNROLL["design"])

    def hot(self):
        def hot_row(k):
            ids = self.cid[pl.ds(k, 1), :]
            hit = iota((256, SLOT), 0) == wide(lax.shift_right_logical(ids, 7), 256)
            self.hot_hi[:, lanes(k)] = jnp.where(hit, 1.0, 0.0).astype(BF16)
            hit = iota((SRC, SLOT), 0) == wide(self.sid[pl.ds(k, 1), :], SRC)
            self.hot_src[:, lanes(k)] = jnp.where(hit, 1.0, 0.0).astype(BF16)

        loop(ROWS, hot_row, UNROLL["hot"])

    def unit_sums(self, out):
        units = self.units

        def unit_row(k):
            low = self.cid[pl.ds(k, 1), :] & 127
            hit = iota((LANES, SLOT), 0) == wide(low, LANES)
            for at in (0, 1):
                value = jnp.where(hit, wide(self.row(10 + at, k), LANES), 0.0)
                units[128 * at : 128 * at + 128, lanes(k)] = value.astype(BF16)

        loop(ROWS, unit_row, UNROLL["units"])
        both = nt_dot(self.hot_hi[...], units[...])
        sums = both[:, :128] + both[:, 128:]
        for s in range(self.ns):
            out[s, 0:8, :] = sums[8 * s : 8 * s + 8]

    def source_normals(self):
        sp, lhs = self.sp, self.lhs

        def source_row(k):
            a = [sp[i, pl.ds(k, 1), :] for i in range(5)]
            self.tiles_a[k] = choose(a, [0, 1, 2, 3, 4, 4, 4, 4])
            parts = []
            for first in (0, 8):
                chosen = (PAIRS + [(4, 4)])[first : first + 8]
                left = choose(a, [p[0] for p in chosen])
                parts.append(left * choose(a, [p[1] for p in chosen]) * wide(self.row(8, k)))
            value = jnp.concatenate(parts, axis=0)
            head, tail = split(value)
            lhs[:16, lanes(k)] = head.astype(BF16)
            lhs[16:, lanes(k)] = tail.astype(BF16)

        loop(ROWS, source_row, UNROLL["source"])
        sums = nt_dot(lhs[...], self.hot_src[...])
        sums = sums[:16] + sums[16:]
        entries = {}
        for at, (i, j) in enumerate(PAIRS):
            entries[i, j] = sums[at : at + 1] + (1.0 if i == j else 0.0)
        low, inv = factor_of(entries)
        keep = [low[i, j] for i, j in PAIRS if i != j] + [inv[i] for i in range(5)]
        for at, value in enumerate(keep):
            self.fac[at : at + 1] = value

    def offsets(self, table):
        head, tail = split(table.T)
        self.cal_t[:128, :] = head.astype(BF16)
        self.cal_t[128:, :] = tail.astype(BF16)

        def offset_row(k):
            got = jnp.dot(self.cal_t[...], self.hot_hi[:, lanes(k)], preferred_element_type=F32)
            got = got[:128] + got[128:]
            hit = iota((LANES, SLOT), 0) == wide(self.cid[pl.ds(k, 1), :] & 127, LANES)
            self.rows_s[13, pl.ds(k, 1), :] = jnp.sum(
                jnp.where(hit, got, 0.0), axis=0, keepdims=True
            )

        loop(ROWS, offset_row, UNROLL["offsets"])

    def remaining(self, table, start):
        out = {}
        for t in TILES:
            i, h = t
            base = tile(self.kb, i, h)
            model = jnp.zeros((8, LANES), F32)
            for j in range(4):
                sum_c = jnp.zeros((8, LANES), F32)
                for c in range(4):
                    part = along(table[8 * i : 8 * i + 8], base + (32 * c + j))
                    sum_c = sum_c + tile(self.ap.at[c], i, h) * part
                model = model + tile(self.rows_s.at[4 + j], i, h) * sum_c
            out[t] = start[t] - model - tile(self.rows_s.at[13], i, h)
        return out

    def less_sources(self, target, params):
        out = {}
        for t in TILES:
            ids = tile(self.sid, *t)
            total = jnp.zeros((8, LANES), F32)
            for i in range(5):
                total = total + tile(self.sp.at[i], *t) * along(wide(params[i]), ids)
            out[t] = target[t] - total
        return out

    def solve_sources(self, target):
        lhs = self.lhs
        self.rows_s[12] = self.rows_s[8] * whole(target)

        def side_row(k):
            value = self.tiles_a[k] * wide(self.row(12, k))
            head, tail = split(value)
            lhs[:16, lanes(k)] = jnp.concatenate([head, tail], axis=0).astype(BF16)

        loop(ROWS, side_row, UNROLL["side"])
        sums = nt_dot(lhs[:16, :], self.hot_src[...])
        sums = sums[:8] + sums[8:]
        kept = [self.fac[at : at + 1] for at in range(15)]
        low = dict(zip([p for p in PAIRS if p[0] != p[1]], kept[:10]))
        return solve_with(low, kept[10:], [sums[i : i + 1] for i in range(5)])

    def right_sides(self, resid, out):
        resid = whole(resid)
        head, tail = split(self.rows_s[8] * resid)
        self.rows_s[10] = head
        self.rows_s[11] = tail
        self.unit_sums(out)
        self.attitude_sides(resid, out)

    def attitude_sides(self, resid, out):
        head, tail = split(self.rows_s[9] * resid)
        left = jnp.concatenate([head, tail], axis=0).astype(BF16)
        for k in range(ROWS):
            got = nt_dot(left, self.dd[k])
            got = got[:, :128] + got[:, 128:]
            got = got[k : k + 1] + got[16 + k : 17 + k]
            out[2 * k, 8:9, :] = got
            out[2 * k + 1, 8:9, :] = got

    def unpack(self, packed):
        lane = iota((ROWS, LANES), 1)
        rows = []
        for g in range(8):
            index = iota((ROWS, LANES), 0) + 16 * g
            ahead = (lane - index) & 127
            place = 32 * (ahead // 32) + 4 * g + ahead % 4
            rows.append(jnp.where(ahead % 32 < 4, along(packed, place), 0.0))
        upper = jnp.concatenate(rows, axis=0)
        r_id, c_id = iota((LANES, LANES), 0), iota((LANES, LANES), 1)
        strict = jnp.where(r_id % 32 == c_id % 32, 0.0, upper)
        full = upper + strict.T + jnp.where(r_id == c_id, 1.0, 0.0)
        order = by_knot((LANES, LANES))
        self.matrix[...] = along(along(full, order).T, order)

    def invert(self, blocks):
        matrix = self.matrix
        lane = iota((ROWS, LANES), 1)
        low = iota((ROWS, LANES), 0)
        lines = {s: matrix[16 * s : 16 * s + 16, :] for s in blocks}
        for j in range(0, ROWS, 2):
            for s in blocks:
                i = 16 * s + j
                line = lines[s]
                first = along(line, jnp.full((ROWS, LANES), i, jnp.int32))
                second = along(line, jnp.full((ROWS, LANES), i + 1, jnp.int32))
                top, side = wide(first[j : j + 1]), wide(first[j + 1 : j + 2])
                end = wide(second[j + 1 : j + 2])
                scale = 1.0 / (top * end - side * side)
                here, there = lane[:8] == i, lane[:8] == i + 1
                upper = jnp.where(here, 1.0, jnp.where(there, 0.0, wide(line[j : j + 1])))
                under = jnp.where(here, 0.0, jnp.where(there, 1.0, wide(line[j + 1 : j + 2])))
                above = (end * upper - side * under) * scale
                below = (top * under - side * upper) * scale
                above = jnp.concatenate([above, above], axis=0)
                below = jnp.concatenate([below, below], axis=0)
                rest = jnp.where((lane == i) | (lane == i + 1), 0.0, line)
                rest = rest - first * above - second * below
                lines[s] = jnp.where(low == j, above, jnp.where(low == j + 1, below, rest))
        zeros = jnp.zeros((ROWS, LANES), F32)
        inner = jnp.concatenate([lines.get(s, zeros) for s in range(8)], axis=0)
        moved = jnp.dot(
            matrix[...], inner, precision=lax.Precision.HIGHEST, preferred_element_type=F32
        )
        kept = jnp.ones((ROWS, LANES), F32)
        for s in blocks:
            kept = jnp.where(lane // 16 == s, 0.0, kept)
        for s in range(8):
            rows = slice(16 * s, 16 * s + 16)
            if s in blocks:
                matrix[rows, :] = lines[s]
            else:
                matrix[rows, :] = matrix[rows, :] * kept - moved[rows]

    def split_inverse(self):
        rest = self.matrix[...]
        for at in range(3):
            head = rest.astype(BF16)
            self.terms[:, 128 * at : 128 * at + 128] = head
            rest = rest - head.astype(F32)

    def advance(self, got, later, offsets, q):
        later[0:8, :] = offsets + got[0:8] * self.inv_den[...]
        right = along(wide(got[8:9]), by_knot((8, LANES)))
        head, rest = split(right)
        middle, tail = split(rest)
        place = iota((8, LANES), 0)
        left = jnp.where(place == 0, head, jnp.where(place == 1, middle, tail))
        left = jnp.concatenate([left, jnp.zeros((8, LANES), F32)], axis=0).astype(BF16)
        every = jnp.dot(left, self.terms[...], preferred_element_type=F32)
        step = every[0:1, 0:128] + (
            (every[0:1, 128:256] + every[1:2, 0:128])
            + (every[0:1, 256:384] + every[1:2, 128:256] + every[2:3, 0:128])
        )
        step = wide(step)
        later[8:9, :] = q + along(step, by_channel((8, LANES)))[0:1]


INPUTS = ["obs", "wobs", "pres", "sp", "ap", "ph", "kb", "sid", "cid", "att", "cal"]
OUTPUTS = ["params_o", "att_o", "cal_o", "res_o"]


def shapes(ns, nt):
    shard = SHARD + 1
    vmem = lambda *shape: pltpu.VMEM(shape, F32)
    out = {
        "rows_s": vmem(14, ROWS, SLOT),
        "dd": pltpu.VMEM((ROWS, 256, SLOT), BF16),
        "hot_hi": pltpu.VMEM((256, OBS), BF16),
        "hot_src": pltpu.VMEM((SRC, OBS), BF16),
        "units": pltpu.VMEM((256, OBS), BF16),
        "lhs": pltpu.VMEM((32, OBS), BF16),
        "cal_t": pltpu.VMEM((256, 256), BF16),
        "matrix": vmem(LANES, LANES),
        "tiles_a": vmem(ROWS, 8, SLOT),
        "terms": pltpu.VMEM((LANES, 3 * LANES), BF16),
        "fac": vmem(16, LANES),
        "inv_den": vmem(8, LANES),
        "qbuf": vmem(nt, 1, LANES),
        "qsend": vmem(1, LANES),
        "ns_s": vmem(ns, 8, LANES),
        "ns_r": vmem(ns, 8, LANES),
        "nt_s": vmem(8, LANES),
        "nt_r": vmem(nt, 8, LANES),
        "ws_s": vmem(ns, 8, LANES),
        "ws_r": vmem(ns, 8, LANES),
        "wt_s": vmem(8, LANES),
        "wt_r": vmem(nt, 8, LANES),
        "pair_r": vmem(2, 8, LANES),
    }
    for n in (2, 3):
        out[f"a{n}s"] = vmem(ns, shard, LANES)
        out[f"a{n}r"] = vmem(ns, shard, LANES)
        out[f"b{n}s"] = vmem(shard, LANES)
        out[f"b{n}r"] = vmem(nt, shard, LANES)
        out[f"c{n}s"] = vmem(shard, LANES)
        out[f"c{n}r"] = vmem(ns, shard, LANES)
    return out


def lanes(k):
    return pl.ds(pl.multiple_of(k * SLOT, SLOT), SLOT)


def ring_order(count):
    return sorted(range(1, count), key=lambda o: -min(o, count - o))


def plane_order(ns):
    far = (0, 1, 2, 1)
    every = [(y, x, c) for y in range(4) for x in range(4) for c in range(ns // 16)]
    return sorted(every, key=lambda o: -4 * (far[o[0]] + far[o[1]]) - o[2])[:-1]


def kernel(ns, nt, *refs):
    count = len(INPUTS)
    given = dict(zip(INPUTS, refs[:count]))
    results = dict(zip(OUTPUTS, refs[count : count + 4]))
    scratch = refs[count + 4 :]
    names = list(shapes(ns, nt))
    d = Device(ns, nt, dict(zip(names, scratch)))
    local = dict(zip(INPUTS, scratch[len(names) : len(names) + count]))
    d.__dict__.update(local)
    send, recv, load = scratch[len(names) + count :]
    me_s, me_t = lax.axis_index("src"), lax.axis_index("tm")
    my_y, my_x, my_c = me_s // 8, lax.rem(me_s // 2, 4), lax.rem(me_s, 2)

    def fetch(name):
        at = INPUTS.index(name)
        return pltpu.make_async_copy(given[name], local[name], load.at[at])

    def ready(*wanted):
        for name in wanted:
            fetch(name).wait()

    in_plane = [
        lax.rem(my_y + y, 4) * 8 + lax.rem(my_x + x, 4) * 2 + lax.rem(my_c + c, 2)
        for y, x, c in plane_order(ns)
    ]
    in_ring = [lax.rem(me_t + o, nt) for o in ring_order(nt)]

    def partners(axis, step):
        for other in in_plane if axis == "src" else in_ring:
            step(other)

    def partners_loop(axis, step):
        size, me = (ns, me_s) if axis == "src" else (nt, me_t)
        loop(size - 1, lambda at: step(lax.rem(me + 1 + at, size)))

    class Exchange:
        def __init__(self, stage, axis, source, target, shards=False):
            self.stage, self.axis, self.source, self.target = stage, axis, source, target
            self.me = me_s if axis == "src" else me_t
            self.shards = shards

        def copy(self, other, slot, sender):
            return pltpu.make_async_remote_copy(
                src_ref=self.source.at[other] if self.shards else self.source,
                dst_ref=self.target.at[slot],
                send_sem=send.at[self.stage, other],
                recv_sem=recv.at[self.stage, sender],
                device_id=(other, me_t) if self.axis == "src" else (me_s, other),
                device_id_type=MESH,
            )

        def start(self):
            partners(self.axis, lambda o: self.copy(o, self.me, self.me).start())
            self.target[self.me] = self.source[self.me] if self.shards else self.source[...]

        def wait(self):
            partners_loop(self.axis, lambda o: self.copy(o, o, o).wait_recv())

        def sent(self):
            partners_loop(self.axis, lambda o: self.copy(o, self.me, self.me).wait_send())

        def total(self):
            return jnp.sum(self.target[...], axis=0)

    barrier = pltpu.get_barrier_semaphore()

    def greet_src(o):
        pl.semaphore_signal(barrier, inc=1, device_id=(o, me_t), device_id_type=MESH)

    def greet_tm(o):
        pl.semaphore_signal(barrier, inc=1, device_id=(me_s, o), device_id_type=MESH)

    partners("tm", greet_tm)
    for name in ("wobs", "pres", "ph", "kb", "ap", "att", "cid", "sid", "sp", "cal", "obs"):
        fetch(name).start()
    partners("src", greet_src)

    first_q = Exchange(0, "tm", d.qsend, d.qbuf)
    normals_s = Exchange(1, "src", d.ns_s, d.ns_r, shards=True)
    normals_t = Exchange(2, "tm", d.nt_s, d.nt_r)
    weights_s = Exchange(3, "src", d.ws_s, d.ws_r, shards=True)
    weights_t = Exchange(4, "tm", d.wt_s, d.wt_r)

    ready("wobs", "pres", "ph")
    d.prepare()
    ready("kb", "ap")
    d.design(d.ns_s)
    ready("att")
    d.qsend[...] = along(wide(d.att[...]), by_channel((8, LANES)))[0:1]

    pl.semaphore_wait(barrier, ns + nt - 2)
    first_q.start()
    normals_s.start()
    ready("cid", "sid")
    d.hot()
    d.unit_sums(d.ws_s)
    weights_s.start()
    ready("sp")
    d.source_normals()
    ready("cal", "obs")
    d.offsets(d.cal[...])
    normals_s.wait()
    d.nt_s[...] = normals_s.total()
    normals_t.start()
    weights_s.wait()
    d.wt_s[...] = weights_s.total()
    weights_t.start()

    def reduce(n):
        at = 5 + 3 * (n - 2)
        return (
            Exchange(at, "src", getattr(d, f"a{n}s"), getattr(d, f"a{n}r"), shards=True),
            Exchange(at + 1, "tm", getattr(d, f"b{n}s"), getattr(d, f"b{n}r")),
            Exchange(at + 2, "src", getattr(d, f"c{n}s"), getattr(d, f"c{n}r")),
        )

    over_src, over_tm, back = reduce(2)
    first_q.wait()
    table = jnp.concatenate([d.qbuf[k] for k in range(nt)], axis=0)
    target = d.remaining(table, {t: tile(d.obs, *t) for t in TILES})
    params = d.solve_sources(target)
    d.right_sides(d.less_sources(target, params), d.a2s)
    over_src.start()

    normals_t.wait()
    half = my_c
    owned = me_s // 2
    d.pair_r[half] = normals_t.total()
    swap = pltpu.make_async_remote_copy(
        src_ref=d.pair_r.at[half],
        dst_ref=d.pair_r.at[half],
        send_sem=send.at[11, 0],
        recv_sem=recv.at[11, 0],
        device_id=(me_s + 1 - 2 * half, me_t),
        device_id_type=MESH,
    )
    swap.start()
    first_q.sent()
    normals_s.sent()
    over_src.wait()
    d.b2s[...] = over_src.total()
    over_tm.start()
    swap.wait()
    d.unpack(jnp.concatenate([d.pair_r[0], d.pair_r[1]], axis=0))
    d.invert((1, 3, 5, 7))
    d.invert((2, 6))
    d.invert((4,))
    d.invert((0,))
    d.split_inverse()
    weights_t.wait()
    d.inv_den[...] = 1.0 / (1.0 + weights_t.total())
    weights_s.sent()
    normals_t.sent()
    weights_t.sent()
    over_src.sent()

    own_cal = pl.ds(pl.multiple_of(8 * me_s, 8), 8)
    over_tm.wait()
    d.advance(over_tm.total(), d.c2s, d.cal[own_cal, :], d.qbuf[owned])
    back.start()
    over_tm.sent()
    back.wait()

    def tables_of(got):
        knots = jnp.concatenate([got[2 * k, 8:9, :] for k in range(nt)], axis=0)
        return knots, got[:, 0:8, :].reshape(ns * 8, LANES)

    table, cal = tables_of(d.c2r)
    d.offsets(cal)
    target = d.remaining(table, {t: tile(d.obs, *t) for t in TILES})
    params = d.solve_sources(target)
    d.right_sides(d.less_sources(target, params), d.a3s)
    back.sent()
    over_src, over_tm, back = reduce(3)
    over_src.start()
    for i in range(5):
        results["params_o"][i : i + 1, :] = params[i]
    over_src.wait()
    d.b3s[...] = over_src.total()
    over_tm.start()
    left = d.less_sources({t: tile(d.obs, *t) for t in TILES}, params)
    over_src.sent()
    over_tm.wait()
    d.advance(over_tm.total(), d.c3s, d.c2s[0:8, :], d.c2s[8:9, :])
    back.start()
    over_tm.sent()
    back.wait()

    table, cal = tables_of(d.c3r)
    results["cal_o"][...] = cal
    d.offsets(cal)
    results["res_o"][...] = whole(d.remaining(table, left))
    results["att_o"][...] = along(wide(d.c3r[2 * me_t, 8:9, :]), by_knot((8, LANES)))[0:1]
    back.sent()


def publish(*arrays):
    def copy(*refs):
        *refs, load = refs
        count = len(refs) // 2
        copies = [
            pltpu.make_async_copy(refs[at], refs[count + at], load.at[at]) for at in range(count)
        ]
        for each in copies:
            each.start()
        for each in copies:
            each.wait()

    return pl.pallas_call(
        copy,
        out_shape=tuple(jax.ShapeDtypeStruct(x.shape, x.dtype) for x in arrays),
        in_specs=[pl.BlockSpec(memory_space=pltpu.VMEM)] * len(arrays),
        out_specs=(pl.BlockSpec(memory_space=pltpu.HBM),) * len(arrays),
        scratch_shapes=[pltpu.SemaphoreType.DMA((len(arrays),))],
        name="publish",
    )(*arrays)


def body(ns, nt, *arrays):
    *arrays, attitude, calibration = arrays
    arrays = [*arrays, attitude.reshape(1, LANES), calibration.reshape(256, LANES)]
    arrays = [pltpu.with_memory_space_constraint(x, pltpu.HBM) for x in arrays]
    vmem = pl.BlockSpec(memory_space=pltpu.VMEM)
    params, att, cal, resid = pl.pallas_call(
        functools.partial(kernel, ns, nt),
        out_shape=(
            pltpu.VMEM((5, SRC), F32),
            pltpu.VMEM((1, LANES), F32),
            pltpu.VMEM((256, LANES), F32),
            pltpu.VMEM((ROWS, SLOT), F32),
        ),
        in_specs=[pl.BlockSpec(memory_space=pltpu.HBM)] * len(arrays),
        out_specs=(vmem,) * 4,
        scratch_shapes=[
            *shapes(ns, nt).values(),
            *(pltpu.VMEM(x.shape, x.dtype) for x in arrays),
            pltpu.SemaphoreType.DMA((12, ns)),
            pltpu.SemaphoreType.DMA((12, ns)),
            pltpu.SemaphoreType.DMA((len(arrays),)),
        ],
        compiler_params=pltpu.CompilerParams(
            collective_id=0, has_side_effects=True, vmem_limit_bytes=VMEM_LIMIT
        ),
        name="astrometric",
    )(*arrays)
    held = [pltpu.with_memory_space_constraint(x, pltpu.VMEM) for x in (params, att, cal, resid)]
    params, att, cal, resid = publish(*held)
    return params, att.reshape(LANES), cal.reshape(-1), resid


def solution(mesh):
    spread = P(None, ("src", "tm"))
    return jax.shard_map(
        functools.partial(body, mesh.shape["src"], mesh.shape["tm"]),
        mesh=mesh,
        in_specs=(
            spread,
            spread,
            spread,
            P(None, None, ("src", "tm")),
            P(None, None, ("src", "tm")),
            spread,
            spread,
            spread,
            spread,
            P("tm"),
            P(),
        ),
        out_specs=(spread, P("tm"), P(), spread),
        check_vma=False,
    )
```

```python
import functools

import jax
import jax.numpy as jnp
from jax import lax
from jax.experimental import pallas as pl
from jax.experimental.pallas import tpu as pltpu
from jax.sharding import PartitionSpec as P

MESH = pl.DeviceIdType.MESH
F32, BF16 = jnp.float32, jnp.bfloat16
ROWS, SLOT, SRC, KNOTS, LANES = 16, 256, 128, 32, 128
OBS = ROWS * SLOT
SHARD = 8
PAIRS = [(i, j) for i in range(5) for j in range(i + 1)]
TILES = [(i, h) for i in range(2) for h in range(2)]
NT = (((1,), (1,)), ((), ()))
VMEM_LIMIT = 48 * 2**20


def iota(shape, axis):
    return lax.broadcasted_iota(jnp.int32, shape, axis)


def loop(count, step, unroll=1):
    def body(at, carry):
        step(at)
        return carry

    lax.fori_loop(0, count, body, 0, unroll=unroll)


def split(value):
    head = value.astype(BF16).astype(F32)
    return head, value - head


def nt_dot(left, right):
    return lax.dot_general(left, right, NT, preferred_element_type=F32)


def whole(tiles):
    return jnp.concatenate(
        [jnp.concatenate([tiles[i, 0], tiles[i, 1]], axis=1) for i in range(2)], axis=0
    )


def tile(ref, i, h):
    return ref[8 * i : 8 * i + 8, 128 * h : 128 * h + 128]


def along(table, places):
    return jnp.take_along_axis(table, places, axis=1)


def wide(row, rows=8):
    return jnp.broadcast_to(row, (rows, row.shape[-1]))


def choose(rows, order):
    place = iota((8, rows[0].shape[-1]), 0)
    out = wide(rows[order[0]])
    for r in range(1, 8):
        if order[r] != order[r - 1]:
            out = jnp.where(place >= r, wide(rows[order[r]]), out)
    return out


def factor_of(entries):
    low, inv = {}, {}
    for i in range(5):
        for j in range(i + 1):
            rest = entries[i, j]
            for o in range(j):
                rest = rest - low[i, o] * low[j, o]
            if i == j:
                inv[i] = 1.0 / jnp.sqrt(rest)
            else:
                low[i, j] = rest * inv[j]
    return low, inv


def solve_with(low, inv, right):
    forward = []
    for i in range(5):
        rest = right[i]
        for o in range(i):
            rest = rest - low[i, o] * forward[o]
        forward.append(rest * inv[i])
    out = [None] * 5
    for i in reversed(range(5)):
        rest = forward[i]
        for o in range(i + 1, 5):
            rest = rest - low[o, i] * out[o]
        out[i] = rest * inv[i]
    return out


def by_channel(shape):
    lane = iota(shape, 1)
    return 4 * (lane % 32) + lane // 32


def by_knot(shape):
    lane = iota(shape, 1)
    return 32 * (lane % 4) + lane // 4


def band_place(shape):
    lane = iota(shape, 1)
    return iota(shape, 0) + 32 * (lane // 32) + lane % 4


UNROLL = {"design": 16, "hot": 16, "units": 16, "source": 16, "side": 16, "offsets": 16}


class Device:
    def __init__(self, ns, nt, refs):
        self.ns, self.nt = ns, nt
        self.__dict__.update(refs)

    def row(self, at, k):
        return self.rows_s[at, pl.ds(k, 1), :]

    def prepare(self):
        rows_s = self.rows_s
        weight = self.pres[...].astype(F32) * self.wobs[...]
        root = jnp.sqrt(weight)
        u = self.ph[...]
        square = u * u
        cube = square * u
        other = 1.0 - u
        basis = [
            other * other * other / 6.0,
            (3.0 * cube - 6.0 * square + 4.0) / 6.0,
            (-3.0 * cube + 3.0 * square + 3.0 * u + 1.0) / 6.0,
            cube / 6.0,
        ]
        for j in range(4):
            rows_s[j] = basis[j] * root
            rows_s[4 + j] = basis[j]
        rows_s[8] = weight
        rows_s[9] = root
        head, tail = split(weight)
        rows_s[10] = head
        rows_s[11] = tail

    def design(self, out):
        spread = band_place((ROWS, LANES))
        group = (iota((ROWS, LANES), 1) % 32) // 4
        dd, ap = self.dd, self.ap

        def build(k):
            knot = iota((KNOTS, SLOT), 0) - wide(self.kb[pl.ds(k, 1), :], KNOTS)
            share = jnp.zeros((KNOTS, SLOT), F32)
            for j in range(4):
                share = jnp.where(knot == j, wide(self.row(j, k), KNOTS), share)
            for c in range(4):
                value = share * wide(ap[c, pl.ds(k, 1), :], KNOTS)
                head, tail = split(value)
                dd[k, 32 * c : 32 * c + 32, :] = head.astype(BF16)
                dd[k, 128 + 32 * c : 160 + 32 * c, :] = tail.astype(BF16)

        def design_row(k):
            both = dd[k]
            full = nt_dot(both, both)
            build(lax.rem(k + 1, ROWS))
            normal = full[:128, :128] + full[:128, 128:] + full[128:, :128] + full[128:, 128:]
            packed = jnp.zeros((ROWS, LANES), F32)
            for g in range(8):
                part = along(normal[16 * g : 16 * g + 16], (spread + 16 * g) & 127)
                packed = jnp.where(group == g, part, packed)
            out[2 * k] = packed[:8]
            out[2 * k + 1] = packed[8:]

        build(0)
        loop(ROWS, design_row, UNROLL["design"])

    def hot(self):
        def hot_row(k):
            ids = self.cid[pl.ds(k, 1), :]
            hit = iota((256, SLOT), 0) == wide(lax.shift_right_logical(ids, 7), 256)
            self.hot_hi[:, lanes(k)] = jnp.where(hit, 1.0, 0.0).astype(BF16)
            hit = iota((SRC, SLOT), 0) == wide(self.sid[pl.ds(k, 1), :], SRC)
            self.hot_src[:, lanes(k)] = jnp.where(hit, 1.0, 0.0).astype(BF16)

        loop(ROWS, hot_row, UNROLL["hot"])

    def unit_sums(self, out):
        units = self.units

        def unit_row(k):
            low = self.cid[pl.ds(k, 1), :] & 127
            hit = iota((LANES, SLOT), 0) == wide(low, LANES)
            for at in (0, 1):
                value = jnp.where(hit, wide(self.row(10 + at, k), LANES), 0.0)
                units[128 * at : 128 * at + 128, lanes(k)] = value.astype(BF16)

        loop(ROWS, unit_row, UNROLL["units"])
        both = nt_dot(self.hot_hi[...], units[...])
        sums = both[:, :128] + both[:, 128:]
        for s in range(self.ns):
            out[s, 0:8, :] = sums[8 * s : 8 * s + 8]

    def source_normals(self):
        sp, lhs = self.sp, self.lhs

        def source_row(k):
            a = [sp[i, pl.ds(k, 1), :] for i in range(5)]
            self.tiles_a[k] = choose(a, [0, 1, 2, 3, 4, 4, 4, 4])
            parts = []
            for first in (0, 8):
                chosen = (PAIRS + [(4, 4)])[first : first + 8]
                left = choose(a, [p[0] for p in chosen])
                parts.append(left * choose(a, [p[1] for p in chosen]) * wide(self.row(8, k)))
            value = jnp.concatenate(parts, axis=0)
            head, tail = split(value)
            lhs[:16, lanes(k)] = head.astype(BF16)
            lhs[16:, lanes(k)] = tail.astype(BF16)

        loop(ROWS, source_row, UNROLL["source"])
        sums = nt_dot(lhs[...], self.hot_src[...])
        sums = sums[:16] + sums[16:]
        entries = {}
        for at, (i, j) in enumerate(PAIRS):
            entries[i, j] = sums[at : at + 1] + (1.0 if i == j else 0.0)
        low, inv = factor_of(entries)
        keep = [low[i, j] for i, j in PAIRS if i != j] + [inv[i] for i in range(5)]
        for at, value in enumerate(keep):
            self.fac[at : at + 1] = value

    def offsets(self, table):
        head, tail = split(table.T)
        self.cal_t[:128, :] = head.astype(BF16)
        self.cal_t[128:, :] = tail.astype(BF16)

        def offset_row(k):
            got = jnp.dot(self.cal_t[...], self.hot_hi[:, lanes(k)], preferred_element_type=F32)
            got = got[:128] + got[128:]
            hit = iota((LANES, SLOT), 0) == wide(self.cid[pl.ds(k, 1), :] & 127, LANES)
            self.rows_s[13, pl.ds(k, 1), :] = jnp.sum(
                jnp.where(hit, got, 0.0), axis=0, keepdims=True
            )

        loop(ROWS, offset_row, UNROLL["offsets"])

    def remaining(self, table, start):
        out = {}
        for t in TILES:
            i, h = t
            base = tile(self.kb, i, h)
            model = jnp.zeros((8, LANES), F32)
            for j in range(4):
                sum_c = jnp.zeros((8, LANES), F32)
                for c in range(4):
                    part = along(table[8 * i : 8 * i + 8], base + (32 * c + j))
                    sum_c = sum_c + tile(self.ap.at[c], i, h) * part
                model = model + tile(self.rows_s.at[4 + j], i, h) * sum_c
            out[t] = start[t] - model - tile(self.rows_s.at[13], i, h)
        return out

    def less_sources(self, target, params):
        out = {}
        for t in TILES:
            ids = tile(self.sid, *t)
            total = jnp.zeros((8, LANES), F32)
            for i in range(5):
                total = total + tile(self.sp.at[i], *t) * along(wide(params[i]), ids)
            out[t] = target[t] - total
        return out

    def solve_sources(self, target):
        lhs = self.lhs
        self.rows_s[12] = self.rows_s[8] * whole(target)

        def side_row(k):
            value = self.tiles_a[k] * wide(self.row(12, k))
            head, tail = split(value)
            lhs[:16, lanes(k)] = jnp.concatenate([head, tail], axis=0).astype(BF16)

        loop(ROWS, side_row, UNROLL["side"])
        sums = nt_dot(lhs[:16, :], self.hot_src[...])
        sums = sums[:8] + sums[8:]
        kept = [self.fac[at : at + 1] for at in range(15)]
        low = dict(zip([p for p in PAIRS if p[0] != p[1]], kept[:10]))
        return solve_with(low, kept[10:], [sums[i : i + 1] for i in range(5)])

    def right_sides(self, resid, out):
        resid = whole(resid)
        head, tail = split(self.rows_s[8] * resid)
        self.rows_s[10] = head
        self.rows_s[11] = tail
        self.unit_sums(out)
        self.attitude_sides(resid, out)

    def attitude_sides(self, resid, out):
        head, tail = split(self.rows_s[9] * resid)
        left = jnp.concatenate([head, tail], axis=0).astype(BF16)
        for k in range(ROWS):
            got = nt_dot(left, self.dd[k])
            got = got[:, :128] + got[:, 128:]
            got = got[k : k + 1] + got[16 + k : 17 + k]
            out[2 * k, 8:9, :] = got
            out[2 * k + 1, 8:9, :] = got

    def unpack(self, packed):
        lane = iota((ROWS, LANES), 1)
        rows = []
        for g in range(8):
            index = iota((ROWS, LANES), 0) + 16 * g
            ahead = (lane - index) & 127
            place = 32 * (ahead // 32) + 4 * g + ahead % 4
            rows.append(jnp.where(ahead % 32 < 4, along(packed, place), 0.0))
        upper = jnp.concatenate(rows, axis=0)
        r_id, c_id = iota((LANES, LANES), 0), iota((LANES, LANES), 1)
        strict = jnp.where(r_id % 32 == c_id % 32, 0.0, upper)
        full = upper + strict.T + jnp.where(r_id == c_id, 1.0, 0.0)
        order = by_knot((LANES, LANES))
        self.matrix[...] = along(along(full, order).T, order)

    def invert(self, blocks):
        matrix = self.matrix
        lane = iota((ROWS, LANES), 1)
        low = iota((ROWS, LANES), 0)
        lines = {s: matrix[16 * s : 16 * s + 16, :] for s in blocks}
        for j in range(0, ROWS, 2):
            for s in blocks:
                i = 16 * s + j
                line = lines[s]
                first = along(line, jnp.full((ROWS, LANES), i, jnp.int32))
                second = along(line, jnp.full((ROWS, LANES), i + 1, jnp.int32))
                top, side = wide(first[j : j + 1]), wide(first[j + 1 : j + 2])
                end = wide(second[j + 1 : j + 2])
                scale = 1.0 / (top * end - side * side)
                here, there = lane[:8] == i, lane[:8] == i + 1
                upper = jnp.where(here, 1.0, jnp.where(there, 0.0, wide(line[j : j + 1])))
                under = jnp.where(here, 0.0, jnp.where(there, 1.0, wide(line[j + 1 : j + 2])))
                above = (end * upper - side * under) * scale
                below = (top * under - side * upper) * scale
                above = jnp.concatenate([above, above], axis=0)
                below = jnp.concatenate([below, below], axis=0)
                rest = jnp.where((lane == i) | (lane == i + 1), 0.0, line)
                rest = rest - first * above - second * below
                lines[s] = jnp.where(low == j, above, jnp.where(low == j + 1, below, rest))
        zeros = jnp.zeros((ROWS, LANES), F32)
        inner = jnp.concatenate([lines.get(s, zeros) for s in range(8)], axis=0)
        moved = jnp.dot(
            matrix[...], inner, precision=lax.Precision.HIGHEST, preferred_element_type=F32
        )
        kept = jnp.ones((ROWS, LANES), F32)
        for s in blocks:
            kept = jnp.where(lane // 16 == s, 0.0, kept)
        for s in range(8):
            rows = slice(16 * s, 16 * s + 16)
            if s in blocks:
                matrix[rows, :] = lines[s]
            else:
                matrix[rows, :] = matrix[rows, :] * kept - moved[rows]

    def split_inverse(self):
        rest = self.matrix[...]
        for at in range(3):
            head = rest.astype(BF16)
            self.terms[:, 128 * at : 128 * at + 128] = head
            rest = rest - head.astype(F32)

    def advance(self, got, later, offsets, q):
        later[0:8, :] = offsets + got[0:8] * self.inv_den[...]
        right = along(wide(got[8:9]), by_knot((8, LANES)))
        head, rest = split(right)
        middle, tail = split(rest)
        place = iota((8, LANES), 0)
        left = jnp.where(place == 0, head, jnp.where(place == 1, middle, tail))
        left = jnp.concatenate([left, jnp.zeros((8, LANES), F32)], axis=0).astype(BF16)
        every = jnp.dot(left, self.terms[...], preferred_element_type=F32)
        step = every[0:1, 0:128] + (
            (every[0:1, 128:256] + every[1:2, 0:128])
            + (every[0:1, 256:384] + every[1:2, 128:256] + every[2:3, 0:128])
        )
        step = wide(step)
        later[8:9, :] = q + along(step, by_channel((8, LANES)))[0:1]


INPUTS = ["obs", "wobs", "pres", "sp", "ap", "ph", "kb", "sid", "cid", "att", "cal"]
OUTPUTS = ["params_o", "att_o", "cal_o", "res_o"]


def shapes(ns, nt):
    shard = SHARD + 1
    vmem = lambda *shape: pltpu.VMEM(shape, F32)
    out = {
        "rows_s": vmem(14, ROWS, SLOT),
        "dd": pltpu.VMEM((ROWS, 256, SLOT), BF16),
        "hot_hi": pltpu.VMEM((256, OBS), BF16),
        "hot_src": pltpu.VMEM((SRC, OBS), BF16),
        "units": pltpu.VMEM((256, OBS), BF16),
        "lhs": pltpu.VMEM((32, OBS), BF16),
        "cal_t": pltpu.VMEM((256, 256), BF16),
        "matrix": vmem(LANES, LANES),
        "tiles_a": vmem(ROWS, 8, SLOT),
        "terms": pltpu.VMEM((LANES, 3 * LANES), BF16),
        "fac": vmem(16, LANES),
        "inv_den": vmem(8, LANES),
        "qbuf": vmem(nt, 1, LANES),
        "qsend": vmem(1, LANES),
        "ns_s": vmem(ns, 8, LANES),
        "ns_r": vmem(ns, 8, LANES),
        "nt_s": vmem(8, LANES),
        "nt_r": vmem(nt, 8, LANES),
        "ws_s": vmem(ns, 8, LANES),
        "ws_r": vmem(ns, 8, LANES),
        "wt_s": vmem(8, LANES),
        "wt_r": vmem(nt, 8, LANES),
        "pair_r": vmem(2, 8, LANES),
    }
    for n in (2, 3):
        out[f"a{n}s"] = vmem(ns, shard, LANES)
        out[f"a{n}r"] = vmem(ns, shard, LANES)
        out[f"b{n}s"] = vmem(shard, LANES)
        out[f"b{n}r"] = vmem(nt, shard, LANES)
        out[f"c{n}s"] = vmem(shard, LANES)
        out[f"c{n}r"] = vmem(ns, shard, LANES)
    return out


def lanes(k):
    return pl.ds(pl.multiple_of(k * SLOT, SLOT), SLOT)


def ring_order(count):
    return sorted(range(1, count), key=lambda o: -min(o, count - o))


def plane_order(ns):
    far = (0, 1, 2, 1)
    every = [(y, x, c) for y in range(4) for x in range(4) for c in range(ns // 16)]
    return sorted(every, key=lambda o: -4 * (far[o[0]] + far[o[1]]) - o[2])[:-1]


def kernel(ns, nt, *refs):
    count = len(INPUTS)
    given = dict(zip(INPUTS, refs[:count]))
    results = dict(zip(OUTPUTS, refs[count : count + 4]))
    scratch = refs[count + 4 :]
    names = list(shapes(ns, nt))
    d = Device(ns, nt, dict(zip(names, scratch)))
    local = dict(zip(INPUTS, scratch[len(names) : len(names) + count]))
    d.__dict__.update(local)
    send, recv, load = scratch[len(names) + count :]
    me_s, me_t = lax.axis_index("src"), lax.axis_index("tm")
    my_y, my_x, my_c = me_s // 8, lax.rem(me_s // 2, 4), lax.rem(me_s, 2)

    def fetch(name):
        at = INPUTS.index(name)
        return pltpu.make_async_copy(given[name], local[name], load.at[at])

    def ready(*wanted):
        for name in wanted:
            fetch(name).wait()

    in_plane = [
        lax.rem(my_y + y, 4) * 8 + lax.rem(my_x + x, 4) * 2 + lax.rem(my_c + c, 2)
        for y, x, c in plane_order(ns)
    ]
    in_ring = [lax.rem(me_t + o, nt) for o in ring_order(nt)]

    def partners(axis, step):
        for other in in_plane if axis == "src" else in_ring:
            step(other)

    def partners_loop(axis, step):
        size, me = (ns, me_s) if axis == "src" else (nt, me_t)
        loop(size - 1, lambda at: step(lax.rem(me + 1 + at, size)))

    class Exchange:
        def __init__(self, stage, axis, source, target, shards=False):
            self.stage, self.axis, self.source, self.target = stage, axis, source, target
            self.me = me_s if axis == "src" else me_t
            self.shards = shards

        def copy(self, other, slot, sender):
            return pltpu.make_async_remote_copy(
                src_ref=self.source.at[other] if self.shards else self.source,
                dst_ref=self.target.at[slot],
                send_sem=send.at[self.stage, other],
                recv_sem=recv.at[self.stage, sender],
                device_id=(other, me_t) if self.axis == "src" else (me_s, other),
                device_id_type=MESH,
            )

        def start(self):
            partners(self.axis, lambda o: self.copy(o, self.me, self.me).start())
            self.target[self.me] = self.source[self.me] if self.shards else self.source[...]

        def wait(self):
            partners_loop(self.axis, lambda o: self.copy(o, o, o).wait_recv())

        def sent(self):
            partners_loop(self.axis, lambda o: self.copy(o, self.me, self.me).wait_send())

        def total(self):
            return jnp.sum(self.target[...], axis=0)

    barrier = pltpu.get_barrier_semaphore()

    def greet_src(o):
        pl.semaphore_signal(barrier, inc=1, device_id=(o, me_t), device_id_type=MESH)

    def greet_tm(o):
        pl.semaphore_signal(barrier, inc=1, device_id=(me_s, o), device_id_type=MESH)

    partners("tm", greet_tm)
    for name in ("wobs", "pres", "ph", "kb", "ap", "att", "cid", "sid", "sp", "cal", "obs"):
        fetch(name).start()
    partners("src", greet_src)

    first_q = Exchange(0, "tm", d.qsend, d.qbuf)
    normals_s = Exchange(1, "src", d.ns_s, d.ns_r, shards=True)
    normals_t = Exchange(2, "tm", d.nt_s, d.nt_r)
    weights_s = Exchange(3, "src", d.ws_s, d.ws_r, shards=True)
    weights_t = Exchange(4, "tm", d.wt_s, d.wt_r)

    ready("wobs", "pres", "ph")
    d.prepare()
    ready("kb", "ap")
    d.design(d.ns_s)
    ready("att")
    d.qsend[...] = along(wide(d.att[...]), by_channel((8, LANES)))[0:1]

    pl.semaphore_wait(barrier, ns + nt - 2)
    first_q.start()
    normals_s.start()
    ready("cid", "sid")
    d.hot()
    d.unit_sums(d.ws_s)
    weights_s.start()
    ready("sp")
    d.source_normals()
    ready("cal", "obs")
    d.offsets(d.cal[...])
    normals_s.wait()
    d.nt_s[...] = normals_s.total()
    normals_t.start()

    def reduce(n):
        at = 5 + 3 * (n - 2)
        return (
            Exchange(at, "src", getattr(d, f"a{n}s"), getattr(d, f"a{n}r"), shards=True),
            Exchange(at + 1, "tm", getattr(d, f"b{n}s"), getattr(d, f"b{n}r")),
            Exchange(at + 2, "src", getattr(d, f"c{n}s"), getattr(d, f"c{n}r")),
        )

    over_src, over_tm, back = reduce(2)
    first_q.wait()
    table = jnp.concatenate([d.qbuf[k] for k in range(nt)], axis=0)
    target = d.remaining(table, {t: tile(d.obs, *t) for t in TILES})
    params = d.solve_sources(target)
    d.right_sides(d.less_sources(target, params), d.a2s)
    over_src.start()
    weights_s.wait()
    d.wt_s[...] = weights_s.total()
    weights_t.start()

    normals_t.wait()
    half = my_c
    owned = me_s // 2
    d.pair_r[half] = normals_t.total()
    swap = pltpu.make_async_remote_copy(
        src_ref=d.pair_r.at[half],
        dst_ref=d.pair_r.at[half],
        send_sem=send.at[11, 0],
        recv_sem=recv.at[11, 0],
        device_id=(me_s + 1 - 2 * half, me_t),
        device_id_type=MESH,
    )
    swap.start()
    first_q.sent()
    normals_s.sent()
    over_src.wait()
    d.b2s[...] = over_src.total()
    over_tm.start()
    swap.wait()
    d.unpack(jnp.concatenate([d.pair_r[0], d.pair_r[1]], axis=0))
    d.invert((1, 3, 5, 7))
    d.invert((2, 6))
    d.invert((4,))
    d.invert((0,))
    d.split_inverse()
    weights_t.wait()
    d.inv_den[...] = 1.0 / (1.0 + weights_t.total())
    weights_s.sent()
    normals_t.sent()
    weights_t.sent()
    over_src.sent()

    own_cal = pl.ds(pl.multiple_of(8 * me_s, 8), 8)
    over_tm.wait()
    d.advance(over_tm.total(), d.c2s, d.cal[own_cal, :], d.qbuf[owned])
    back.start()
    over_tm.sent()
    back.wait()

    def tables_of(got):
        knots = jnp.concatenate([got[2 * k, 8:9, :] for k in range(nt)], axis=0)
        return knots, got[:, 0:8, :].reshape(ns * 8, LANES)

    table, cal = tables_of(d.c2r)
    d.offsets(cal)
    target = d.remaining(table, {t: tile(d.obs, *t) for t in TILES})
    params = d.solve_sources(target)
    d.right_sides(d.less_sources(target, params), d.a3s)
    returned = back
    over_src, over_tm, back = reduce(3)
    over_src.start()
    returned.sent()
    for i in range(5):
        results["params_o"][i : i + 1, :] = params[i]
    over_src.wait()
    d.b3s[...] = over_src.total()
    over_tm.start()
    left = d.less_sources({t: tile(d.obs, *t) for t in TILES}, params)
    over_src.sent()
    over_tm.wait()
    d.advance(over_tm.total(), d.c3s, d.c2s[0:8, :], d.c2s[8:9, :])
    back.start()
    over_tm.sent()
    back.wait()

    table, cal = tables_of(d.c3r)
    results["cal_o"][...] = cal
    d.offsets(cal)
    results["res_o"][...] = whole(d.remaining(table, left))
    results["att_o"][...] = along(wide(d.c3r[2 * me_t, 8:9, :]), by_knot((8, LANES)))[0:1]
    back.sent()


def publish(*arrays):
    def copy(*refs):
        *refs, load = refs
        count = len(refs) // 2
        copies = [
            pltpu.make_async_copy(refs[at], refs[count + at], load.at[at]) for at in range(count)
        ]
        for each in copies:
            each.start()
        for each in copies:
            each.wait()

    return pl.pallas_call(
        copy,
        out_shape=tuple(jax.ShapeDtypeStruct(x.shape, x.dtype) for x in arrays),
        in_specs=[pl.BlockSpec(memory_space=pltpu.VMEM)] * len(arrays),
        out_specs=(pl.BlockSpec(memory_space=pltpu.HBM),) * len(arrays),
        scratch_shapes=[pltpu.SemaphoreType.DMA((len(arrays),))],
        name="publish",
    )(*arrays)


def body(ns, nt, *arrays):
    *arrays, attitude, calibration = arrays
    arrays = [*arrays, attitude.reshape(1, LANES), calibration.reshape(256, LANES)]
    arrays = [pltpu.with_memory_space_constraint(x, pltpu.HBM) for x in arrays]
    vmem = pl.BlockSpec(memory_space=pltpu.VMEM)
    params, att, cal, resid = pl.pallas_call(
        functools.partial(kernel, ns, nt),
        out_shape=(
            pltpu.VMEM((5, SRC), F32),
            pltpu.VMEM((1, LANES), F32),
            pltpu.VMEM((256, LANES), F32),
            pltpu.VMEM((ROWS, SLOT), F32),
        ),
        in_specs=[pl.BlockSpec(memory_space=pltpu.HBM)] * len(arrays),
        out_specs=(vmem,) * 4,
        scratch_shapes=[
            *shapes(ns, nt).values(),
            *(pltpu.VMEM(x.shape, x.dtype) for x in arrays),
            pltpu.SemaphoreType.DMA((12, ns)),
            pltpu.SemaphoreType.DMA((12, ns)),
            pltpu.SemaphoreType.DMA((len(arrays),)),
        ],
        compiler_params=pltpu.CompilerParams(
            collective_id=0, has_side_effects=True, vmem_limit_bytes=VMEM_LIMIT
        ),
        name="astrometric",
    )(*arrays)
    held = [pltpu.with_memory_space_constraint(x, pltpu.VMEM) for x in (params, att, cal, resid)]
    params, att, cal, resid = publish(*held)
    return params, att.reshape(LANES), cal.reshape(-1), resid


def solution(mesh):
    spread = P(None, ("src", "tm"))
    return jax.shard_map(
        functools.partial(body, mesh.shape["src"], mesh.shape["tm"]),
        mesh=mesh,
        in_specs=(
            spread,
            spread,
            spread,
            P(None, None, ("src", "tm")),
            P(None, None, ("src", "tm")),
            spread,
            spread,
            spread,
            spread,
            P("tm"),
            P(),
        ),
        out_specs=(spread, P("tm"), P(), spread),
        check_vma=False,
    )
```
